128 devices in a mesh: frame: 64 (over y, x, z_lo, core), tok: 2 (over z_hi).
Axes of the slice: x: 4, y: 4, z: 4 (z_hi: 2, z_lo: 2; z = z_hi * 2 + z_lo), core: 2. Of those that a mesh axis runs over, the one named last changes fastest.
Arguments:
- tokens: bfloat16 [32768, 1536], P(('frame', 'tok')), may hold values from -6 to 6
- modulation: float32 [64, 3, 1536], P('frame'), may hold values from -3 to 3
- qkv_weight: bfloat16 [3, 1536, 1536], P(None, None, 'tok'), may hold values from -1 to 1
- out_weight: bfloat16 [1536, 1536], P('tok'), may hold values from -0.15625 to 0.15625
- qk_gain: float32 [2, 1536], P(None, 'tok'), may hold values from 0.5 to 6
- text: bfloat16 [256, 1536], replicated, may hold values from -6 to 6
- text_count: int32 [1], replicated, may hold values from 64 to 256
- window: int32 [64, 2], P('frame'), may hold values from 0 to 64, as said below
Outputs:
- mixed: bfloat16 [32768, 1536], P(('frame', 'tok'))
The draws below stay inside these ranges and needn't reach their ends.
Inputs may be any that keep to these rules, and one draw needn't show every extreme that they name: `window`: each row is f+1-8 <= start < end <= f+1 for frame f; the last frame has start = 56 and end = 64.
All inputs are finite; a program needn't handle non-finite values.
Results may differ from the reference program's by a relative error of at most 0.012.
The reference program's roundings to bfloat16 on the way (of `hidden`, `weights` and `attended`) count: a program that leaves them out, or rounds other values in their place, can miss the bound.
Values may be sent and summed in bfloat16 or wider, within the bound.
A program may use at most 128 MiB of HBM per device.

```python
import jax
import jax.numpy as jnp
from jax import lax

D = 1536
HEADS = 12
HEAD_DIM = 128
TEXT = 256
WIN = 8
FRAME_TOK = 512
FRAMES = 64
TOKENS = 32768


def draw_tokens(key, part):
    key = jax.random.fold_in(key, 3)
    first = jax.random.fold_in(key, 0)
    base = jnp.clip(jax.random.normal(first, (TOKENS, D), jnp.float32), -6.0, 6.0)
    return base.astype(jnp.bfloat16)


def draw_modulation(key, part):
    key = jax.random.fold_in(key, 5)
    first, second, third = jax.random.split(key, 3)
    shift = jnp.clip(0.5 * jax.random.normal(first, (FRAMES, 1, D), jnp.float32), -2.0, 2.0)
    stretch = jnp.clip(0.3 * jax.random.normal(second, (FRAMES, 1, D), jnp.float32), -0.9, 0.9)
    gate = jnp.clip(jax.random.normal(third, (FRAMES, 1, D), jnp.float32), -3.0, 3.0)
    return jnp.concatenate([shift, stretch, gate], axis=1)


def draw_qkv_weight(key, part):
    key = jax.random.fold_in(key, 7)
    first = jax.random.fold_in(key, 0)
    base = jnp.clip(jax.random.normal(first, (3, D, D), jnp.float32), -5.0, 5.0) * D ** (-0.5)
    return base.astype(jnp.bfloat16)


def draw_qk_gain(key, part):
    key = jax.random.fold_in(key, 9)
    gain = jnp.exp(jax.random.uniform(key, (2, D), jnp.float32, -0.35, 0.45))
    return gain


def draw_window(key, part):
    key = jax.random.fold_in(key, 11)
    first, second = jax.random.split(key)
    frame_ids = jnp.arange(FRAMES, dtype=jnp.int32)
    drop = jax.random.randint(first, (FRAMES,), 0, 2, dtype=jnp.int32)
    finish = jnp.maximum(frame_ids + 1 - drop, 1)
    span = jax.random.randint(second, (FRAMES,), 1, WIN + 1, dtype=jnp.int32)
    begin = jnp.maximum(finish - span, jnp.maximum(frame_ids + 1 - WIN, 0))
    last = frame_ids == FRAMES - 1
    begin = jnp.where(last, FRAMES - WIN, begin)
    finish = jnp.where(last, FRAMES, finish)
    return jnp.stack([begin, finish], axis=1).astype(jnp.int32)


def block_levels(key, shape, cuts, least, largest):
    def one(dim, parts):
        heights = jax.random.uniform(jax.random.fold_in(jax.random.fold_in(key, 6), dim), (parts,), jnp.float32, least / len(cuts), largest / len(cuts))
        return jnp.repeat(jnp.exp(heights), shape[dim] // parts).reshape((-1,) + (1,) * (len(shape) - dim - 1))

    factor_of = one(*cuts[0])
    for cut in cuts[1:]:
        factor_of = factor_of * one(*cut)
    return factor_of


def scatter_about(stream_key, shape, scale, most, shards=(), kind=jnp.bfloat16):
    result = jax.random.normal(stream_key, shape, jnp.float32) * scale
    if len(shards) > 0:
        result = block_levels(stream_key, shape, shards, -0.22, 0.18) * result
    return jnp.clip(result, min=-most, max=most).astype(kind)


def setup_inputs(seed: int = 0) -> dict:
    keys = jax.random.split(jax.random.key(seed), 9)
    return {
        "tokens": draw_tokens(jax.random.fold_in(keys[8], 71), 0),
        "modulation": draw_modulation(jax.random.fold_in(keys[8], 71), 0),
        "qkv_weight": draw_qkv_weight(jax.random.fold_in(keys[8], 71), 0),
        "out_weight": scatter_about(keys[3], (D, D), D ** -0.5, 0.15625, ((0, 2),)),
        "qk_gain": draw_qk_gain(jax.random.fold_in(keys[8], 71), 0),
        "text": scatter_about(keys[5], (TEXT, D), 1.0, 6.0),
        "text_count": jax.random.randint(keys[6], (1,), TEXT // 4, TEXT + 1).astype(jnp.int32),
        "window": draw_window(jax.random.fold_in(keys[8], 71), 0),
    }


EPSILON = 1e-06

def head_norm(projected, gain):
    shaped = projected.reshape(projected.shape[0], -1, HEAD_DIM)
    mean_square = lax.optimization_barrier(jnp.mean(shaped * shaped, axis=-1, keepdims=True))
    return (shaped * lax.rsqrt(mean_square + EPSILON) * gain.reshape(1, -1, HEAD_DIM)).astype(jnp.bfloat16)

def modulate(rows, frame_mod):
    center = lax.optimization_barrier(jnp.mean(rows, axis=-1, keepdims=True))
    spread = lax.optimization_barrier(jnp.mean(jnp.square(rows - center), axis=-1, keepdims=True))
    normed = (rows - center) * lax.rsqrt(spread + EPSILON)
    return (normed * (1.0 + frame_mod[1]) + frame_mod[0]).astype(jnp.bfloat16)

def reference(tokens, modulation, qkv_weight, out_weight, qk_gain, text, text_count, window):
    wide = qkv_weight.astype(jnp.float32)
    framed = tokens.reshape(FRAMES, FRAME_TOK, D).astype(jnp.float32)

    def project(inputs):
        rows, frame_mod = inputs
        hidden = modulate(rows, frame_mod).astype(jnp.float32)
        triple = jnp.einsum('td,cde->cte', hidden, wide)
        return (head_norm(triple[0], qk_gain[0]), head_norm(triple[1], qk_gain[1]), triple[2].reshape(FRAME_TOK, HEADS, HEAD_DIM).astype(jnp.bfloat16))
    queries, keys_all, values_all = lax.map(project, (framed, modulation))
    text_pair = jnp.einsum('td,cde->cte', text.astype(jnp.float32), wide[1:])
    text_keys = head_norm(text_pair[0], qk_gain[1])
    text_values = text_pair[1].reshape(TEXT, HEADS, HEAD_DIM).astype(jnp.bfloat16)
    text_valid = jnp.arange(TEXT, dtype=jnp.int32) < text_count[0]
    padding = jnp.zeros((WIN - 1, FRAME_TOK, HEADS, HEAD_DIM), jnp.bfloat16)
    keys_pad = jnp.concatenate([padding, keys_all], axis=0)
    values_pad = jnp.concatenate([padding, values_all], axis=0)
    scale = HEAD_DIM ** (-0.5)

    def attend(inputs):
        frame_id, query_block, bounds = inputs
        key_win = lax.dynamic_slice_in_dim(keys_pad, frame_id.astype(jnp.int32), WIN, 0).reshape(WIN * FRAME_TOK, HEADS, HEAD_DIM)
        value_win = lax.dynamic_slice_in_dim(values_pad, frame_id.astype(jnp.int32), WIN, 0).reshape(WIN * FRAME_TOK, HEADS, HEAD_DIM)
        source = frame_id - (WIN - 1) + jnp.arange(WIN, dtype=jnp.int32)
        frame_ok = (source >= bounds[0]) & (source < bounds[1])
        valid = jnp.concatenate([text_valid, jnp.repeat(frame_ok, FRAME_TOK)])
        key_rows = jnp.concatenate([text_keys, key_win], axis=0).astype(jnp.float32)
        value_rows = jnp.concatenate([text_values, value_win], axis=0).astype(jnp.float32)
        scores = jnp.einsum('qhd,khd->qhk', query_block.astype(jnp.float32), key_rows) * scale
        scores = jnp.where(valid[None, None, :], scores, -1e+30)
        highest = lax.optimization_barrier(jnp.max(scores, axis=-1, keepdims=True))
        weights = jnp.exp(scores - highest)
        total = lax.optimization_barrier(jnp.sum(weights, axis=-1))
        summed = jnp.einsum('qhk,khd->qhd', weights.astype(jnp.bfloat16).astype(jnp.float32), value_rows)
        return (summed / total[..., None]).astype(jnp.bfloat16).reshape(FRAME_TOK, D)
    attended = lax.map(attend, (jnp.arange(FRAMES, dtype=jnp.int32), queries, window))
    update = jnp.dot(attended.reshape(TOKENS, D), out_weight, preferred_element_type=jnp.float32)
    gate = jnp.repeat(modulation[:, 2], FRAME_TOK, axis=0)
    return (tokens.astype(jnp.float32) + gate * update).astype(jnp.bfloat16)
```

```python
import functools

import jax
import jax.numpy as jnp
from jax import lax
from jax.experimental import pallas as pl
from jax.experimental.pallas import tpu as pltpu
from jax.sharding import PartitionSpec as P

HEAD_DIM = 128
GROUP = 3
EPSILON = 1e-06
LOW = -1e30
SCALE = HEAD_DIM ** (-0.5) * 1.4426950408889634
MESH = pl.DeviceIdType.MESH


def dot(a, b):
    return jnp.dot(a, b, preferred_element_type=jnp.float32)


def dot_t(a, b):
    return lax.dot_general(a, b, (((1,), (1,)), ((), ())), preferred_element_type=jnp.float32)


def kernel(
    groups,
    tokens, mod, w_hbm, ow_hbm, gain, text, count, window,
    out,
    mine, hid, w, ow, kv, tk, q, acc, top, tot, att, attin,
    w_sem, hid_send, hid_relay, hid_recv, kv_send, kv_recv, ow_send, ow_recv, att_send, att_recv,
):
    rows, width = tokens.shape
    part_rows = mine.shape[0] // 2
    cols = GROUP * HEAD_DIM
    fi = lax.axis_index("frame")
    tok = lax.axis_index("tok")
    line = fi // 4
    zlo = (fi // 2) % 2
    core = fi % 2
    z = 2 * tok + zlo
    partner = 1 - core

    def dev(line_, z_, core_):
        return (4 * line_ + 2 * (z_ % 2) + core_, z_ // 2)

    def w_copy(c):
        return pltpu.make_async_copy(
            w_hbm.at[c, :, pl.ds(pl.multiple_of(zlo * cols, 128), cols)], w.at[c], w_sem.at[c]
        )

    def ow_copy():
        return pltpu.make_async_copy(ow_hbm, ow.at[tok], w_sem.at[3])

    for c in (1, 2, 0):
        w_copy(c).start()

    barrier = pltpu.get_barrier_semaphore()

    def greet(device):
        pl.semaphore_signal(barrier, inc=1, device_id=device, device_id_type=MESH)

    for c in range(2):
        for d in range(1, 4):
            greet(dev(line, (z + d) % 4, c))
    greet(dev(line, z, partner))

    @pl.when(line > 0)
    def _():
        for c in range(2):
            greet(dev(line - 1, z, c))

    @pl.when(line < groups - 1)
    def _():
        for c in range(2):
            greet(dev(line + 1, z, c))

    step_rows = 32

    def norm_rows(step, carry):
        at = pl.ds(pl.multiple_of(step * step_rows, step_rows), step_rows)
        x = tokens[at, :].astype(jnp.float32)
        center = jnp.mean(x, axis=-1, keepdims=True)
        x = x - center
        spread = jnp.mean(x * x, axis=-1, keepdims=True)
        x = x * lax.rsqrt(spread + EPSILON)
        mine[at, :] = (x * (1.0 + mod[0, 1:2, :]) + mod[0, 0:1, :]).astype(jnp.bfloat16)
        return carry

    lax.fori_loop(0, rows // step_rows, norm_rows, 0)
    mine[pl.ds(rows, 16), :] = jnp.full((16, width), window[0, 0], jnp.int32).astype(jnp.float32).astype(jnp.bfloat16)
    mine[pl.ds(rows + 16, 16), :] = jnp.full((16, width), window[0, 1], jnp.int32).astype(jnp.float32).astype(jnp.bfloat16)

    pl.semaphore_wait(barrier, 7 + jnp.where(line > 0, 2, 0) + jnp.where(line < groups - 1, 2, 0))

    def part_at(part):
        return pl.ds(pl.multiple_of(part * part_rows, 16), part_rows)

    def hid_copy(which, part):
        device = (dev(line, (z + 1) % 4, zlo), dev(line, (z + 3) % 4, zlo), dev(line, z, zlo))[which]
        return pltpu.make_async_remote_copy(
            src_ref=mine.at[part_at(part), :],
            dst_ref=hid.at[core, tok, part_at(part), :],
            send_sem=hid_send.at[which, part],
            recv_sem=hid_recv.at[core, tok, part],
            device_id=device,
            device_id_type=MESH,
        )

    hid_copy(0, 0).start()
    hid_copy(1, 1).start()
    hid_copy(0, 1).start()
    hid_copy(1, 0).start()

    @pl.when(core != zlo)
    def _():
        hid_copy(2, 0).start()
        hid_copy(2, 1).start()

    @pl.when(core == zlo)
    def _():
        hid[core, tok] = mine[...]

    def hid_wait(p, h, part):
        pltpu.make_async_remote_copy(
            src_ref=mine.at[part_at(part), :],
            dst_ref=hid.at[p, h, part_at(part), :],
            send_sem=hid_send.at[0, part],
            recv_sem=hid_recv.at[p, h, part],
            device_id=dev(line, z, partner),
            device_id_type=MESH,
        ).wait_recv()

    def hid_pass(p, h):
        part = jnp.where((2 * h + core + 1) % 4 == z, 0, 1)
        to = (z + 1 + 2 * part) % 4
        return pltpu.make_async_remote_copy(
            src_ref=hid.at[p, h, part_at(part), :],
            dst_ref=hid.at[p, h, part_at(part), :],
            send_sem=hid_relay.at[p, h],
            recv_sem=hid_recv.at[p, h, part],
            device_id=dev(line, to, core),
            device_id_type=MESH,
        )

    def kv_at(g, o, h):
        return kv.at[g, o, :, pl.ds(pl.multiple_of(h * rows, rows), rows), :]

    def kv_copy(kind, g, o, h, to_g, device):
        return pltpu.make_async_remote_copy(
            src_ref=kv_at(g, o, h),
            dst_ref=kv_at(to_g, o, h),
            send_sem=kv_send.at[kind, g, o, h],
            recv_sem=kv_recv.at[to_g, o, h],
            device_id=device,
            device_id_type=MESH,
        )

    def kv_wait(g, o, h):
        kv_copy(0, g, o, h, g, dev(line, z, partner)).wait_recv()

    def own_next(p, h):
        return kv_copy(0, 2, 2 * core + p, h, 1, dev(line + 1, z, core))

    def own_share(p, h):
        return kv_copy(1, 2, 2 * core + p, h, 2, dev(line, z, partner))

    def pass_next(p, h):
        o = 2 * core + p
        return kv_copy(0, 1, o, h, 0, dev(line + 1, z, jnp.where(o == 3, 1, 0)))

    def pass_share(p, h):
        return kv_copy(1, 1, 2 * core + p, h, 1, dev(line, z, partner))

    def old_share(h):
        return kv_copy(1, 0, 3, h, 0, dev(line, z, partner))

    has_prev = line > 0
    has_next = line < groups - 1

    def head_norm(x, which, hd):
        scaled = x * lax.rsqrt(jnp.mean(x * x, axis=-1, keepdims=True) + EPSILON)
        at = pl.ds(pl.multiple_of(zlo * cols + hd * HEAD_DIM, 128), HEAD_DIM)
        return (scaled * gain[which:which + 1, at]).astype(jnp.bfloat16)

    def block_of(k):
        return (core + k) % 2, (tok + k // 2) % 2

    def own_block(k, carry):
        p, h = block_of(k)

        @pl.when(jnp.logical_or(core != zlo, k > 0))
        def _():
            hid_wait(p, h, 0)
            hid_wait(p, h, 1)

            @pl.when(core != zlo)
            def _():
                hid_pass(p, h).start()

        x = hid[p, h, :rows, :]
        at = pl.ds(pl.multiple_of(h * rows, rows), rows)
        o = 2 * core + p
        keys = dot(x, w[1])
        values = dot(x, w[2])
        for hd in range(GROUP):
            lanes = slice(hd * HEAD_DIM, (hd + 1) * HEAD_DIM)
            kv[2, o, hd, at, :] = head_norm(keys[:, lanes], 1, hd)
            kv[2, o, GROUP + hd, at, :] = values[:, lanes].astype(jnp.bfloat16)

        @pl.when(has_next)
        def _():
            own_next(p, h).start()

        @pl.when(core == 0)
        def _():
            own_share(p, h).start()

        queries = dot(x, w[0])
        for hd in range(GROUP):
            lanes = slice(hd * HEAD_DIM, (hd + 1) * HEAD_DIM)
            q[p, hd, at, :] = head_norm(queries[:, lanes], 0, hd)
        return carry

    def pass_block(k, carry):
        p, h = block_of(k)

        @pl.when(has_prev)
        def _():
            kv_wait(1, 2 * core + p, h)

            @pl.when(jnp.logical_and(has_next, core + p > 0))
            def _():
                pass_next(p, h).start()

            pass_share(p, h).start()

        return carry

    for c in (1, 2, 0):
        w_copy(c).wait()
    ow_copy().start()
    lax.fori_loop(0, 2, own_block, 0)

    text_keys = dot(text[...], w[1])
    text_values = dot(text[...], w[2])
    for hd in range(GROUP):
        lanes = slice(hd * HEAD_DIM, (hd + 1) * HEAD_DIM)
        tk[hd] = head_norm(text_keys[:, lanes], 1, hd)
        tk[GROUP + hd] = text_values[:, lanes].astype(jnp.bfloat16)

    lax.fori_loop(0, 2, pass_block, 0)
    lax.fori_loop(2, 4, own_block, 0)

    def ow_cross():
        at = pl.ds(pl.multiple_of(core * cols, 128), cols)
        return pltpu.make_async_remote_copy(
            src_ref=ow.at[tok, at, :],
            dst_ref=ow.at[tok, at, :],
            send_sem=ow_send.at[0],
            recv_sem=ow_recv.at[0],
            device_id=dev(line, 3 - z, core),
            device_id_type=MESH,
        )

    def ow_share(which):
        at = pl.ds(pl.multiple_of(which * cols, 128), cols)
        return pltpu.make_async_remote_copy(
            src_ref=ow.at[1 - tok, at, :],
            dst_ref=ow.at[1 - tok, at, :],
            send_sem=ow_send.at[1],
            recv_sem=ow_recv.at[1],
            device_id=dev(line, z, partner),
            device_id_type=MESH,
        )

    def ow_wait_cross():
        at = pl.ds(pl.multiple_of(core * cols, 128), cols)
        pltpu.make_async_remote_copy(
            src_ref=ow.at[tok, at, :],
            dst_ref=ow.at[1 - tok, at, :],
            send_sem=ow_send.at[0],
            recv_sem=ow_recv.at[0],
            device_id=dev(line, 3 - z, core),
            device_id_type=MESH,
        ).wait_recv()

    ow_copy().wait()
    ow_cross().start()

    def text_attend(t, carry):
        p, hd = t // GROUP, t % GROUP
        s = dot_t(q[p, hd], tk[hd])
        s = jnp.where(lax.broadcasted_iota(jnp.int32, s.shape, 1) < count[0], s, LOW)
        m = jnp.broadcast_to(jnp.max(s, axis=1, keepdims=True) * SCALE, (2 * rows, HEAD_DIM))
        e = [jnp.exp2(s[:, n:n + HEAD_DIM] * SCALE - m) for n in range(0, s.shape[1], HEAD_DIM)]
        top[p, hd] = m
        tot[p, hd] = functools.reduce(jnp.add, e)
        acc[p, hd] = dot(jnp.concatenate([x.astype(jnp.bfloat16) for x in e], axis=1), tk[GROUP + hd])
        return carry

    def frame_attend(g, o):
        frame = (4 * (line - 2) + 4 * g + o).astype(jnp.float32)

        def step(t, carry):
            p, hd = t // GROUP, t % GROUP
            first = hid[p, 0, rows:rows + 16, :HEAD_DIM].astype(jnp.float32)[:1]
            end = hid[p, 0, rows + 16:rows + 32, :HEAD_DIM].astype(jnp.float32)[:1]
            inside = jnp.logical_and(frame >= first, frame < end)
            s = dot_t(q[p, hd], kv[g, o, hd])
            m = jnp.broadcast_to(jnp.max(s, axis=1, keepdims=True) * SCALE, (2 * rows, HEAD_DIM))
            before = top[p, hd]
            m = jnp.maximum(before, jnp.where(inside, m, LOW))
            top[p, hd] = m
            shrink = jnp.exp2(before - m)
            m = jnp.where(inside, m, -LOW)
            e = [jnp.exp2(s[:, n:n + HEAD_DIM] * SCALE - m) for n in range(0, s.shape[1], HEAD_DIM)]
            tot[p, hd] = tot[p, hd] * shrink + functools.reduce(jnp.add, e)
            acc[p, hd] = acc[p, hd] * shrink + dot(
                jnp.concatenate([x.astype(jnp.bfloat16) for x in e], axis=1), kv[g, o, GROUP + hd]
            )
            return carry

        return step

    lax.fori_loop(0, 2 * GROUP, text_attend, 0)
    lax.fori_loop(0, 2 * GROUP, frame_attend(2, 2 * core), 0)
    lax.fori_loop(2, 4, pass_block, 0)
    lax.fori_loop(GROUP, 2 * GROUP, frame_attend(2, 2 * core + 1), 0)

    def slot(j):
        s = 1 + 2 * core + j
        return s // 4, s % 4

    def slot_wait(g, o):
        @pl.when(jnp.logical_or(g != 1, o // 2 != core))
        def _():
            for h in range(2):
                half = h if h == 0 else 1
                kv_wait(g, o, half)

                @pl.when(jnp.logical_and(g == 0, core == 1))
                def _():
                    old_share(half).start()

    def older(i, carry):
        j = 6 - i
        g, o = slot(j)

        @pl.when(line + g >= 2)
        def _():
            slot_wait(g, o)
            lax.fori_loop(0, 2 * GROUP, frame_attend(g, o), 0)

        return carry

    lax.fori_loop(0, 6, older, 0)
    ow_wait_cross()
    ow_share(core).start()
    g0, o0 = slot(0)

    @pl.when(line >= 2)
    def _():
        slot_wait(g0, o0)
        lax.fori_loop(0, GROUP, frame_attend(g0, o0), 0)

    def att_copy(p, h):
        return pltpu.make_async_remote_copy(
            src_ref=att.at[p, h],
            dst_ref=attin.at[z],
            send_sem=att_send.at[p, h],
            recv_sem=att_recv.at[z],
            device_id=dev(line, 2 * h + core, p),
            device_id_type=MESH,
        )

    def is_here(p, h):
        return jnp.logical_and(2 * h + core == z, p == core)

    for p in range(2):
        for hd in range(GROUP):
            lanes = slice(hd * HEAD_DIM, (hd + 1) * HEAD_DIM)
            total = jnp.sum(tot[p, hd], axis=1, keepdims=True)
            result = (acc[p, hd] / total).astype(jnp.bfloat16)
            for h in range(2):
                att[p, h, :, lanes] = result[h * rows:(h + 1) * rows]
        for h in range(2):
            here = is_here(p, h)

            @pl.when(jnp.logical_not(here))
            def _():
                att_copy(p, h).start()

            @pl.when(here)
            def _():
                attin[z] = att[p, h]

    ow_share(partner).wait_recv()
    for s in range(4):
        @pl.when(jnp.logical_not(jnp.logical_and(s == z, core == zlo)))
        def _():
            pltpu.make_async_remote_copy(
                src_ref=att.at[0, 0],
                dst_ref=attin.at[s],
                send_sem=att_send.at[0, 0],
                recv_sem=att_recv.at[s],
                device_id=dev(line, z, partner),
                device_id_type=MESH,
            ).wait_recv()

    step_cols = 256

    def project(n, carry):
        at = pl.ds(pl.multiple_of(n * step_cols, step_cols), step_cols)
        update = dot(attin[0], ow[0, :cols, at])
        update += dot(attin[1], ow[0, cols:, at])
        update += dot(attin[2], ow[1, :cols, at])
        update += dot(attin[3], ow[1, cols:, at])
        out[:, at] = (tokens[:, at].astype(jnp.float32) + mod[0, 2:3, at] * update).astype(jnp.bfloat16)
        return carry

    lax.fori_loop(0, width // step_cols, project, 0)

    for part in range(2):
        hid_copy(0, part).wait_send()
        hid_copy(1, part).wait_send()

        @pl.when(core != zlo)
        def _():
            hid_copy(2, part).wait_send()

    ow_cross().wait_send()
    ow_share(core).wait_send()

    def drain(k, carry):
        p, h = k % 2, k // 2

        @pl.when(core != zlo)
        def _():
            hid_pass(p, h).wait_send()

        @pl.when(has_next)
        def _():
            own_next(p, h).wait_send()

        @pl.when(core == 0)
        def _():
            own_share(p, h).wait_send()

        @pl.when(has_prev)
        def _():
            @pl.when(jnp.logical_and(has_next, core + p > 0))
            def _():
                pass_next(p, h).wait_send()

            pass_share(p, h).wait_send()

        @pl.when(jnp.logical_not(is_here(p, h)))
        def _():
            att_copy(p, h).wait_send()

        @pl.when(jnp.logical_and(jnp.logical_and(line >= 2, core == 1), p == 0))
        def _():
            old_share(h).wait_send()

        return carry

    lax.fori_loop(0, 4, drain, 0)


def shards(groups, tokens, modulation, qkv_weight, out_weight, qk_gain, text, text_count, window):
    rows, width = tokens.shape
    text_rows = text.shape[0]
    cols = GROUP * HEAD_DIM
    bf16, f32 = jnp.bfloat16, jnp.float32
    vmem = pl.BlockSpec(memory_space=pltpu.VMEM)
    smem = pl.BlockSpec(memory_space=pltpu.SMEM)
    hbm = pl.BlockSpec(memory_space=pl.ANY)
    dma = pltpu.SemaphoreType.DMA
    return pl.pallas_call(
        functools.partial(kernel, groups),
        out_shape=jax.ShapeDtypeStruct((rows, width), bf16),
        in_specs=[vmem, vmem, hbm, hbm, vmem, vmem, smem, smem],
        out_specs=vmem,
        scratch_shapes=[
            pltpu.VMEM((rows + 32, width), bf16),
            pltpu.VMEM((2, 2, rows + 32, width), bf16),
            pltpu.VMEM((3, width, cols), bf16),
            pltpu.VMEM((2, width // 2, width), bf16),
            pltpu.VMEM((3, 4, 2 * GROUP, 2 * rows, HEAD_DIM), bf16),
            pltpu.VMEM((2 * GROUP, text_rows, HEAD_DIM), bf16),
            pltpu.VMEM((2, GROUP, 2 * rows, HEAD_DIM), bf16),
            pltpu.VMEM((2, GROUP, 2 * rows, HEAD_DIM), f32),
            pltpu.VMEM((2, GROUP, 2 * rows, HEAD_DIM), f32),
            pltpu.VMEM((2, GROUP, 2 * rows, HEAD_DIM), f32),
            pltpu.VMEM((2, 2, rows, cols), bf16),
            pltpu.VMEM((4, rows, cols), bf16),
            dma((4,)),
            dma((3, 2)),
            dma((2, 2)),
            dma((2, 2, 2)),
            dma((2, 3, 4, 2)),
            dma((3, 4, 2)),
            dma((2,)),
            dma((2,)),
            dma((2, 2)),
            dma((4,)),
        ],
        compiler_params=pltpu.CompilerParams(
            collective_id=0, has_side_effects=True, vmem_limit_bytes=58 * 1024 * 1024
        ),
        cost_estimate=pl.CostEstimate(flops=13_000_000_000, bytes_accessed=12_000_000, transcendentals=13_400_000),
    )(tokens, modulation, qkv_weight, out_weight, qk_gain, text, text_count, window)


def solution(mesh):
    in_specs = (
        P(("frame", "tok"), None),
        P("frame", None, None),
        P(None, None, "tok"),
        P("tok", None),
        P(None, "tok"),
        P(),
        P(),
        P("frame", None),
    )
    out_specs = P(("frame", "tok"), None)
    return jax.shard_map(
        functools.partial(shards, mesh.shape["frame"] // 4),
        mesh=mesh, in_specs=in_specs, out_specs=out_specs, check_vma=False,
    )
```

```python
import functools

import jax
import jax.numpy as jnp
from jax import lax
from jax.experimental import pallas as pl
from jax.experimental.pallas import tpu as pltpu
from jax.sharding import PartitionSpec as P

HEAD_DIM = 128
GROUP = 3
EPSILON = 1e-06
LOW = -1e30
SCALE = HEAD_DIM ** (-0.5) * 1.4426950408889634
MESH = pl.DeviceIdType.MESH


def dot(a, b):
    return jnp.dot(a, b, preferred_element_type=jnp.float32)


def dot_t(a, b):
    return lax.dot_general(a, b, (((1,), (1,)), ((), ())), preferred_element_type=jnp.float32)


def kernel(
    groups,
    tokens, mod, w_hbm, ow_hbm, gain, text, count, window,
    out,
    mine, hid, win_mine, win, w, ow, kv, tk, q, acc, top, tot, att, attin,
    w_sem, hid_send, hid_relay, hid_recv, win_send, win_recv, kv_send, kv_recv, ow_send, ow_recv, att_send, att_recv,
):
    rows, width = tokens.shape
    half = rows // 2
    cols = GROUP * HEAD_DIM
    depth = max(groups // 4, 1)
    fi = lax.axis_index("frame")
    tok = lax.axis_index("tok")
    line = fi // 4
    x = line % 4
    y = line // 4
    zlo = (fi // 2) % 2
    core = fi % 2
    z = 2 * tok + zlo
    partner = 1 - core
    near = core == zlo

    def dev(line_, z_, core_):
        return (4 * line_ + 2 * (z_ % 2) + core_, z_ // 2)

    def remote(src, dst, send, recv, device):
        return pltpu.make_async_remote_copy(
            src_ref=src, dst_ref=dst, send_sem=send, recv_sem=recv, device_id=device, device_id_type=MESH
        )

    beside = dev(line, z, partner)
    has_prev = line > 0
    has_next = line < groups - 1
    has_next2 = line < groups - 2
    back_line = jnp.where(x == 0, line + 3, line - 1)
    back_from = jnp.where(x == 3, line - 3, line + 1)
    has_back = jnp.logical_and(back_from >= 0, back_from < groups - 2)

    def w_copy(c):
        return pltpu.make_async_copy(
            w_hbm.at[c, :, pl.ds(pl.multiple_of(zlo * cols, 128), cols)], w.at[c], w_sem.at[c]
        )

    def ow_copy():
        return pltpu.make_async_copy(ow_hbm, ow.at[tok], w_sem.at[3])

    for c in (1, 2, 0):
        w_copy(c).start()

    barrier = pltpu.get_barrier_semaphore()

    def greet(device):
        pl.semaphore_signal(barrier, inc=1, device_id=device, device_id_type=MESH)

    for c in range(2):
        for d in range(1, 4):
            greet(dev(line, (z + d) % 4, c))
    greet(beside)

    for d in range(1, depth):
        greet(dev(4 * ((y + d) % depth) + x, z, core))

    def greet_line(line_):
        for c in range(2):
            greet(dev(line_, z, c))

    @pl.when(has_prev)
    def _():
        greet_line(line - 1)

    @pl.when(has_next)
    def _():
        greet_line(line + 1)

    @pl.when(has_next2)
    def _():
        greet(dev(back_line, z, core))

    @pl.when(has_back)
    def _():
        greet(dev(back_from, z, core))
        greet_line(back_from + 2)

    old_x = (line + 2) % 4
    old_relay = jnp.where(old_x == 0, line + 1, line - 3)

    @pl.when(line >= 2)
    def _():
        greet_line(old_relay)

    def ones(flag, n):
        return jnp.where(flag, n, 0)

    greeted = (
        7 + depth - 1 + ones(has_prev, 2) + ones(has_next, 2) + ones(has_next2, 1) + ones(has_back, 3) + ones(line >= 2, 2)
    )

    step_rows = 32

    def norm_rows(step, carry):
        at = pl.ds(pl.multiple_of(step * step_rows, step_rows), step_rows)
        v = tokens[at, :].astype(jnp.float32)
        v = v - jnp.mean(v, axis=-1, keepdims=True)
        spread = jnp.mean(v * v, axis=-1, keepdims=True)
        v = v * lax.rsqrt(spread + EPSILON)
        mine[at, :] = (v * (1.0 + mod[0, 1:2, :]) + mod[0, 0:1, :]).astype(jnp.bfloat16)
        return carry

    lax.fori_loop(0, rows // step_rows, norm_rows, 0)
    for n in range(2):
        win_mine[n] = jnp.full((8, HEAD_DIM), window[0, n], jnp.int32).astype(jnp.float32)

    pl.semaphore_wait(barrier, greeted)

    def half_at(part):
        return pl.ds(pl.multiple_of(part * half, half), half)

    def hid_copy(which, part):
        device = (dev(line, (z + 1) % 4, zlo), dev(line, (z + 3) % 4, zlo), dev(line, z, zlo))[which]
        return remote(
            mine.at[half_at(part), :], hid.at[core, tok, half_at(part), :],
            hid_send.at[which, part], hid_recv.at[core, tok, part], device,
        )

    def win_copy(which):
        device = (dev(line, (z + 1) % 4, zlo), dev(line, z, zlo))[which]
        return remote(win_mine, win.at[core], win_send.at[which], win_recv.at[core], device)

    def hid_wait(p, h, part):
        remote(
            mine.at[half_at(part), :], hid.at[p, h, half_at(part), :],
            hid_send.at[0, part], hid_recv.at[p, h, part], beside,
        ).wait_recv()

    def first_part(h):
        return jnp.where((2 * h + core + 1) % 4 == z, 0, 1)

    def hid_pass(p, h):
        part = first_part(h)
        return remote(
            hid.at[p, h, half_at(part), :], hid.at[p, h, half_at(part), :],
            hid_relay.at[p, h], hid_recv.at[p, h, part], dev(line, (z + 1 + 2 * part) % 4, core),
        )

    hid_copy(0, 0).start()
    hid_copy(1, 1).start()

    @pl.when(jnp.logical_not(near))
    def _():
        hid_copy(2, 0).start()
        hid_copy(2, 1).start()
        win_copy(1).start()

    win_copy(0).start()

    @pl.when(near)
    def _():
        hid[core, tok] = mine[...]
        win[core] = win_mine[...]

    def sub_rows(h, part):
        return pl.ds(pl.multiple_of((2 * h + part) * half, half), half)

    def kv_copy(kind, g, o, h, part, to_g, device):
        at = sub_rows(h, part)
        return remote(
            kv.at[g, o, :, at, :], kv.at[to_g, o, :, at, :],
            kv_send.at[kind, o, 2 * h + part], kv_recv.at[to_g, o, 2 * h + part], device,
        )

    def kv_wait(g, o, h, part):
        kv_copy(0, g, o, h, part, g, beside).wait_recv()

    def old_core(o):
        return jnp.where(o == 3, 1, 0)

    def own_next(o, h, part):
        return kv_copy(0, 2, o, h, part, 1, dev(line + 1, z, core))

    def own_back(o, h, part):
        return kv_copy(1, 2, o, h, part, 3, dev(back_line, z, core))

    def own_share(o, h, part):
        return kv_copy(2, 2, o, h, part, 2, beside)

    def pass_next(o, h, part):
        return kv_copy(3, 1, o, h, part, 0, dev(line + 1, z, old_core(o)))

    def pass_share(o, h, part):
        return kv_copy(4, 1, o, h, part, 1, beside)

    def pass_back(o, h, part):
        return kv_copy(5, 3, o, h, part, 0, dev(back_from + 2, z, old_core(o)))

    def old_share(h, part):
        return kv_copy(6, 0, 3, h, part, 0, beside)

    def sub_of(k):
        h = jnp.where(near, (tok + k // 4) % 2, k % 2)
        p = jnp.where(near, (core + k // 2) % 2, (k // 2) % 2)
        part = jnp.where(near, k % 2, (first_part(h) + k // 4) % 2)
        return p, h, part

    def by_next(k):
        return jnp.logical_and(k < 4, k % 2 == 0)

    def own_goes(k, o):
        return has_next, jnp.logical_and(jnp.logical_and(has_next2, o > 0), jnp.logical_not(by_next(k))), core == 0

    def pass_goes(k, o):
        return (
            jnp.logical_and(jnp.logical_and(has_prev, has_next), jnp.logical_and(o > 0, by_next(k))),
            jnp.logical_and(has_back, jnp.logical_and(o > 0, jnp.logical_not(by_next(k)))),
        )

    def head_norm(v, which, hd):
        scaled = v * lax.rsqrt(jnp.mean(v * v, axis=-1, keepdims=True) + EPSILON)
        at = pl.ds(pl.multiple_of(zlo * cols + hd * HEAD_DIM, 128), HEAD_DIM)
        return (scaled * gain[which:which + 1, at]).astype(jnp.bfloat16)

    def own_pair(kk, carry):
        subs = [sub_of(2 * kk), sub_of(2 * kk + 1)]
        p = subs[0][0]
        o = 2 * core + p
        for _, h, part in subs:
            @pl.when(jnp.logical_or(jnp.logical_not(near), kk > 0))
            def _():
                hid_wait(p, h, part)

                @pl.when(jnp.logical_and(jnp.logical_not(near), kk < 2))
                def _():
                    hid_pass(p, h).start()

        v = jnp.concatenate([hid[p, h, half_at(part), :] for _, h, part in subs], axis=0)
        keys = dot(v, w[1])
        values = dot(v, w[2])
        for hd in range(GROUP):
            lanes = slice(hd * HEAD_DIM, (hd + 1) * HEAD_DIM)
            normed = head_norm(keys[:, lanes], 1, hd)
            plain = values[:, lanes].astype(jnp.bfloat16)
            for n, (_, h, part) in enumerate(subs):
                kv[2, o, hd, sub_rows(h, part), :] = normed[n * half:(n + 1) * half]
                kv[2, o, GROUP + hd, sub_rows(h, part), :] = plain[n * half:(n + 1) * half]
        for n, (_, h, part) in enumerate(subs):
            for flag, copy in zip(own_goes(2 * kk + n, o), (own_next, own_back, own_share)):
                @pl.when(flag)
                def _():
                    copy(o, h, part).start()

        queries = dot(v, w[0])
        for hd in range(GROUP):
            lanes = slice(hd * HEAD_DIM, (hd + 1) * HEAD_DIM)
            normed = head_norm(queries[:, lanes], 0, hd)
            for n, (_, h, part) in enumerate(subs):
                q[p, hd, sub_rows(h, part), :] = normed[n * half:(n + 1) * half]
        return carry

    def pass_sub(k, carry):
        p, h, part = sub_of(k)
        o = 2 * core + p
        go_next, go_back = pass_goes(k, o)

        @pl.when(has_prev)
        def _():
            kv_wait(1, o, h, part)

            @pl.when(go_next)
            def _():
                pass_next(o, h, part).start()

            pass_share(o, h, part).start()

        @pl.when(go_back)
        def _():
            kv_wait(3, o, h, part)
            pass_back(o, h, part).start()

        return carry

    for c in (1, 2, 0):
        w_copy(c).wait()
    ow_copy().start()
    lax.fori_loop(0, 2, own_pair, 0)

    text_keys = dot(text[...], w[1])
    text_values = dot(text[...], w[2])
    for hd in range(GROUP):
        lanes = slice(hd * HEAD_DIM, (hd + 1) * HEAD_DIM)
        tk[hd] = head_norm(text_keys[:, lanes], 1, hd)
        tk[GROUP + hd] = text_values[:, lanes].astype(jnp.bfloat16)

    lax.fori_loop(0, 2, pass_sub, 0)
    hid_copy(0, 0).wait_send()
    hid_copy(1, 1).wait_send()
    hid_copy(0, 1).start()
    hid_copy(1, 0).start()
    lax.fori_loop(2, 4, pass_sub, 0)
    lax.fori_loop(2, 4, own_pair, 0)

    piece_rows = width // 2 // (2 * depth)

    def piece(n):
        return pl.ds(pl.multiple_of(n * piece_rows, 16), piece_rows)

    my_piece = 2 * y + core

    def ow_cross(which=None):
        of = tok if which is None else which
        return remote(
            ow.at[tok, piece(my_piece), :], ow.at[of, piece(my_piece), :],
            ow_send.at[0], ow_recv.at[my_piece], dev(line, 3 - z, core),
        )

    def ow_along(d):
        return remote(
            ow.at[1 - tok, piece(my_piece), :], ow.at[1 - tok, piece(my_piece), :],
            ow_send.at[d], ow_recv.at[my_piece], dev(4 * ((y + d) % depth) + x, z, core),
        )

    def ow_share(d, which):
        n = 2 * ((y + d) % depth) + which
        return remote(
            ow.at[1 - tok, piece(n), :], ow.at[1 - tok, piece(n), :],
            ow_send.at[depth + d], ow_recv.at[n], beside,
        )

    ow_copy().wait()
    ow_cross().start()

    @pl.when(near)
    def _():
        win_copy(0).wait_send()

    @pl.when(jnp.logical_not(near))
    def _():
        win_copy(0).wait_send()
        win_copy(1).wait_send()

    def win_wait(p):
        remote(win_mine, win.at[p], win_send.at[0], win_recv.at[p], beside).wait_recv()

    @pl.when(near)
    def _():
        win_wait(partner)

    @pl.when(jnp.logical_not(near))
    def _():
        win_wait(0)
        win_wait(1)

    def text_attend(t, carry):
        p, hd = t // GROUP, t % GROUP
        s = dot_t(q[p, hd], tk[hd])
        s = jnp.where(lax.broadcasted_iota(jnp.int32, s.shape, 1) < count[0], s, LOW)
        m = jnp.broadcast_to(jnp.max(s, axis=1, keepdims=True) * SCALE, (2 * rows, HEAD_DIM))
        e = [jnp.exp2(s[:, n:n + HEAD_DIM] * SCALE - m) for n in range(0, s.shape[1], HEAD_DIM)]
        top[p, hd] = m
        tot[p, hd] = functools.reduce(jnp.add, e)
        acc[p, hd] = dot(jnp.concatenate([v.astype(jnp.bfloat16) for v in e], axis=1), tk[GROUP + hd])
        return carry

    def frame_attend(g, o):
        frame = (4 * (line - 2) + 4 * g + o).astype(jnp.float32)

        def step(t, carry):
            p, hd = t // GROUP, t % GROUP
            inside = jnp.logical_and(frame >= win[p, 0, :1], frame < win[p, 1, :1])
            s = dot_t(q[p, hd], kv[g, o, hd])
            m = jnp.broadcast_to(jnp.max(s, axis=1, keepdims=True) * SCALE, (2 * rows, HEAD_DIM))
            before = top[p, hd]
            m = jnp.maximum(before, jnp.where(inside, m, LOW))
            top[p, hd] = m
            shrink = jnp.exp2(before - m)
            m = jnp.where(inside, m, -LOW)
            e = [jnp.exp2(s[:, n:n + HEAD_DIM] * SCALE - m) for n in range(0, s.shape[1], HEAD_DIM)]
            tot[p, hd] = tot[p, hd] * shrink + functools.reduce(jnp.add, e)
            acc[p, hd] = acc[p, hd] * shrink + dot(
                jnp.concatenate([v.astype(jnp.bfloat16) for v in e], axis=1), kv[g, o, GROUP + hd]
            )
            return carry

        return step

    lax.fori_loop(0, 2 * GROUP, text_attend, 0)
    pass_sub(4, 0)
    lax.fori_loop(0, GROUP, frame_attend(2, 2 * core), 0)
    pass_sub(5, 0)
    lax.fori_loop(GROUP, 2 * GROUP, frame_attend(2, 2 * core), 0)
    pass_sub(6, 0)
    lax.fori_loop(GROUP, 2 * GROUP, frame_attend(2, 2 * core + 1), 0)
    pass_sub(7, 0)

    def slot(j):
        s = 1 + 2 * core + j
        return s // 4, s % 4

    def slot_wait(g, o):
        for n in range(4):
            h, part = n // 2, n % 2
            kv_wait(g, o, h, part)

            @pl.when(jnp.logical_and(g == 0, core == 1))
            def _():
                old_share(h, part).start()

    def newer(i, carry):
        g, o = slot(6 - i)

        @pl.when(jnp.logical_and(g > 0, line + g >= 2))
        def _():
            @pl.when(jnp.logical_or(g != 1, o // 2 != core))
            def _():
                slot_wait(g, o)

            lax.fori_loop(0, 2 * GROUP, frame_attend(g, o), 0)

        return carry

    lax.fori_loop(0, 6, newer, 0)

    ow_cross(1 - tok).wait_recv()
    for d in range(1, depth):
        ow_along(d).start()
    ow_share(0, core).start()

    def att_copy(p, h):
        return remote(
            att.at[p, h], attin.at[z], att_send.at[p, h], att_recv.at[z], dev(line, 2 * h + core, p)
        )

    def is_here(p, h):
        return jnp.logical_and(2 * h + core == z, p == core)

    def finish(p):
        for hd in range(GROUP):
            lanes = slice(hd * HEAD_DIM, (hd + 1) * HEAD_DIM)
            total = jnp.sum(tot[p, hd], axis=1, keepdims=True)
            result = (acc[p, hd] / total).astype(jnp.bfloat16)
            for h in range(2):
                att[p, h, :, lanes] = result[h * rows:(h + 1) * rows]
        for h in range(2):
            here = is_here(p, h)

            @pl.when(jnp.logical_not(here))
            def _():
                att_copy(p, h).start()

            @pl.when(here)
            def _():
                attin[z] = att[p, h]

    for j in (2, 1):
        @pl.when(jnp.logical_and(line >= 2, core == 0))
        def _():
            g, o = 0, 1 + j
            slot_wait(g, o)
            lax.fori_loop(GROUP, 2 * GROUP, frame_attend(g, o), 0)

    finish(1)

    @pl.when(jnp.logical_and(line >= 2, core == 0))
    def _():
        slot_wait(0, 1)
        for o in (3, 2, 1):
            lax.fori_loop(0, GROUP, frame_attend(0, o), 0)

    @pl.when(jnp.logical_and(line >= 2, core == 1))
    def _():
        slot_wait(0, 3)
        lax.fori_loop(0, GROUP, frame_attend(0, 3), 0)

    finish(0)

    for d in range(1, depth):
        n = 2 * ((y + d) % depth) + core
        remote(
            ow.at[1 - tok, piece(n), :], ow.at[1 - tok, piece(n), :], ow_send.at[d], ow_recv.at[n], beside
        ).wait_recv()
        ow_share(d, core).start()
    for d in range(depth):
        ow_share(d, partner).wait_recv()

    for s in range(4):
        @pl.when(jnp.logical_not(jnp.logical_and(s == z, near)))
        def _():
            remote(att.at[0, 0], attin.at[s], att_send.at[0, 0], att_recv.at[s], beside).wait_recv()

    step_cols = 256

    def project(n, carry):
        at = pl.ds(pl.multiple_of(n * step_cols, step_cols), step_cols)
        update = dot(attin[0], ow[0, :cols, at])
        update += dot(attin[1], ow[0, cols:, at])
        update += dot(attin[2], ow[1, :cols, at])
        update += dot(attin[3], ow[1, cols:, at])
        out[:, at] = (tokens[:, at].astype(jnp.float32) + mod[0, 2:3, at] * update).astype(jnp.bfloat16)
        return carry

    lax.fori_loop(0, width // step_cols, project, 0)

    hid_copy(0, 1).wait_send()
    hid_copy(1, 0).wait_send()

    @pl.when(jnp.logical_not(near))
    def _():
        hid_copy(2, 0).wait_send()
        hid_copy(2, 1).wait_send()
        for p in range(2):
            for h in range(2):
                hid_pass(p, h).wait_send()

    ow_cross().wait_send()
    for d in range(1, depth):
        ow_along(d).wait_send()
    for d in range(depth):
        ow_share(d, core).wait_send()

    for p in range(2):
        for h in range(2):
            @pl.when(jnp.logical_not(is_here(p, h)))
            def _():
                att_copy(p, h).wait_send()

    def drain(k, carry):
        p, h, part = sub_of(k)
        o = 2 * core + p
        for flag, copy in zip(own_goes(k, o), (own_next, own_back, own_share)):
            @pl.when(flag)
            def _():
                copy(o, h, part).wait_send()

        for flag, copy in zip(pass_goes(k, o), (pass_next, pass_back)):
            @pl.when(flag)
            def _():
                copy(o, h, part).wait_send()

        @pl.when(has_prev)
        def _():
            pass_share(o, h, part).wait_send()

        @pl.when(jnp.logical_and(jnp.logical_and(line >= 2, core == 1), p == 0))
        def _():
            old_share(h, part).wait_send()

        return carry

    lax.fori_loop(0, 8, drain, 0)


def shards(groups, tokens, modulation, qkv_weight, out_weight, qk_gain, text, text_count, window):
    rows, width = tokens.shape
    text_rows = text.shape[0]
    cols = GROUP * HEAD_DIM
    depth = max(groups // 4, 1)
    bf16, f32 = jnp.bfloat16, jnp.float32
    vmem = pl.BlockSpec(memory_space=pltpu.VMEM)
    smem = pl.BlockSpec(memory_space=pltpu.SMEM)
    hbm = pl.BlockSpec(memory_space=pl.ANY)
    dma = pltpu.SemaphoreType.DMA
    return pl.pallas_call(
        functools.partial(kernel, groups),
        out_shape=jax.ShapeDtypeStruct((rows, width), bf16),
        in_specs=[vmem, vmem, hbm, hbm, vmem, vmem, smem, smem],
        out_specs=vmem,
        scratch_shapes=[
            pltpu.VMEM((rows, width), bf16),
            pltpu.VMEM((2, 2, rows, width), bf16),
            pltpu.VMEM((2, 8, HEAD_DIM), f32),
            pltpu.VMEM((2, 2, 8, HEAD_DIM), f32),
            pltpu.VMEM((3, width, cols), bf16),
            pltpu.VMEM((2, width // 2, width), bf16),
            pltpu.VMEM((4, 4, 2 * GROUP, 2 * rows, HEAD_DIM), bf16),
            pltpu.VMEM((2 * GROUP, text_rows, HEAD_DIM), bf16),
            pltpu.VMEM((2, GROUP, 2 * rows, HEAD_DIM), bf16),
            pltpu.VMEM((2, GROUP, 2 * rows, HEAD_DIM), f32),
            pltpu.VMEM((2, GROUP, 2 * rows, HEAD_DIM), f32),
            pltpu.VMEM((2, GROUP, 2 * rows, HEAD_DIM), f32),
            pltpu.VMEM((2, 2, rows, cols), bf16),
            pltpu.VMEM((4, rows, cols), bf16),
            dma((4,)),
            dma((3, 2)),
            dma((2, 2)),
            dma((2, 2, 2)),
            dma((2,)),
            dma((2,)),
            dma((7, 4, 4)),
            dma((4, 4, 4)),
            dma((2 * depth,)),
            dma((2 * depth,)),
            dma((2, 2)),
            dma((4,)),
        ],
        compiler_params=pltpu.CompilerParams(
            collective_id=0, has_side_effects=True, vmem_limit_bytes=58 * 1024 * 1024
        ),
        cost_estimate=pl.CostEstimate(flops=13_000_000_000, bytes_accessed=12_000_000, transcendentals=13_400_000),
    )(tokens, modulation, qkv_weight, out_weight, qk_gain, text, text_count, window)


def solution(mesh):
    in_specs = (
        P(("frame", "tok"), None),
        P("frame", None, None),
        P(None, None, "tok"),
        P("tok", None),
        P(None, "tok"),
        P(),
        P(),
        P("frame", None),
    )
    out_specs = P(("frame", "tok"), None)
    return jax.shard_map(
        functools.partial(shards, mesh.shape["frame"] // 4),
        mesh=mesh, in_specs=in_specs, out_specs=out_specs, check_vma=False,
    )
```

```python
import functools

import jax
import jax.numpy as jnp
from jax import lax
from jax.experimental import pallas as pl
from jax.experimental.pallas import tpu as pltpu
from jax.sharding import PartitionSpec as P

HEAD_DIM = 128
GROUP = 3
EPSILON = 1e-06
LOW = -1e30
SCALE = HEAD_DIM ** (-0.5) * 1.4426950408889634
MESH = pl.DeviceIdType.MESH


def dot(a, b):
    return jnp.dot(a, b, preferred_element_type=jnp.float32)


def dot_t(a, b):
    return lax.dot_general(a, b, (((1,), (1,)), ((), ())), preferred_element_type=jnp.float32)


def kernel(
    groups,
    tokens, mod, w_hbm, ow_hbm, gain, text, count, window,
    out,
    mine, hid, win_mine, win, w, ow, kv, tk, q, acc, top, tot, att, attin,
    w_sem, hid_send, hid_relay, hid_recv, win_send, win_recv, kv_send, kv_recv, ow_send, ow_recv, att_send, att_recv,
):
    rows, width = tokens.shape
    half = rows // 2
    cols = GROUP * HEAD_DIM
    depth = max(groups // 4, 1)
    fi = lax.axis_index("frame")
    tok = lax.axis_index("tok")
    line = fi // 4
    x = line % 4
    y = line // 4
    zlo = (fi // 2) % 2
    core = fi % 2
    z = 2 * tok + zlo
    partner = 1 - core
    near = core == zlo

    def dev(line_, z_, core_):
        return (4 * line_ + 2 * (z_ % 2) + core_, z_ // 2)

    def remote(src, dst, send, recv, device):
        return pltpu.make_async_remote_copy(
            src_ref=src, dst_ref=dst, send_sem=send, recv_sem=recv, device_id=device, device_id_type=MESH
        )

    beside = dev(line, z, partner)
    has_prev = line > 0
    has_next = line < groups - 1
    has_next2 = line < groups - 2
    back_line = jnp.where(x == 1, line - 1, line + 3)
    back_from = jnp.where(x == 0, line + 1, line - 3)
    has_back = jnp.logical_and(back_from >= 0, back_from < groups - 2)

    def w_copy(c):
        return pltpu.make_async_copy(
            w_hbm.at[c, :, pl.ds(pl.multiple_of(zlo * cols, 128), cols)], w.at[c], w_sem.at[c]
        )

    def ow_copy():
        return pltpu.make_async_copy(ow_hbm, ow.at[tok], w_sem.at[3])

    for c in (1, 2, 0):
        w_copy(c).start()

    barrier = pltpu.get_barrier_semaphore()

    def greet(device):
        pl.semaphore_signal(barrier, inc=1, device_id=device, device_id_type=MESH)

    for c in range(2):
        for d in range(1, 4):
            greet(dev(line, (z + d) % 4, c))
    greet(beside)

    for d in range(1, depth):
        greet(dev(4 * ((y + d) % depth) + x, z, core))

    def greet_line(line_):
        for c in range(2):
            greet(dev(line_, z, c))

    @pl.when(has_prev)
    def _():
        greet_line(line - 1)

    @pl.when(has_next)
    def _():
        greet_line(line + 1)

    @pl.when(has_next2)
    def _():
        greet(dev(back_line, z, core))

    @pl.when(has_back)
    def _():
        greet(dev(back_from, z, core))
        greet_line(back_from + 2)

    old_x = (line + 2) % 4
    old_relay = jnp.where(old_x == 1, line - 3, line + 1)

    @pl.when(line >= 2)
    def _():
        greet_line(old_relay)

    def ones(flag, n):
        return jnp.where(flag, n, 0)

    greeted = (
        7 + depth - 1 + ones(has_prev, 2) + ones(has_next, 2) + ones(has_next2, 1) + ones(has_back, 3) + ones(line >= 2, 2)
    )

    step_rows = 32

    def norm_rows(step, carry):
        at = pl.ds(pl.multiple_of(step * step_rows, step_rows), step_rows)
        v = tokens[at, :].astype(jnp.float32)
        v = v - jnp.mean(v, axis=-1, keepdims=True)
        spread = jnp.mean(v * v, axis=-1, keepdims=True)
        v = v * lax.rsqrt(spread + EPSILON)
        mine[at, :] = (v * (1.0 + mod[0, 1:2, :]) + mod[0, 0:1, :]).astype(jnp.bfloat16)
        return carry

    lax.fori_loop(0, rows // step_rows, norm_rows, 0)
    for n in range(2):
        win_mine[n] = jnp.full((8, HEAD_DIM), window[0, n], jnp.int32).astype(jnp.float32)

    pl.semaphore_wait(barrier, greeted)

    def half_at(part):
        return pl.ds(pl.multiple_of(part * half, half), half)

    def hid_copy(which, part):
        device = (dev(line, (z + 1) % 4, zlo), dev(line, (z + 3) % 4, zlo), dev(line, z, zlo))[which]
        return remote(
            mine.at[half_at(part), :], hid.at[core, tok, half_at(part), :],
            hid_send.at[which, part], hid_recv.at[core, tok, part], device,
        )

    def win_copy(which):
        device = (dev(line, (z + 1) % 4, zlo), dev(line, z, zlo))[which]
        return remote(win_mine, win.at[core], win_send.at[which], win_recv.at[core], device)

    def hid_wait(p, h, part):
        remote(
            mine.at[half_at(part), :], hid.at[p, h, half_at(part), :],
            hid_send.at[0, part], hid_recv.at[p, h, part], beside,
        ).wait_recv()

    def first_part(h):
        return jnp.where((2 * h + core + 1) % 4 == z, 0, 1)

    def hid_pass(p, h):
        part = first_part(h)
        return remote(
            hid.at[p, h, half_at(part), :], hid.at[p, h, half_at(part), :],
            hid_relay.at[p, h], hid_recv.at[p, h, part], dev(line, (z + 1 + 2 * part) % 4, core),
        )

    hid_copy(0, 0).start()
    hid_copy(1, 1).start()

    @pl.when(jnp.logical_not(near))
    def _():
        hid_copy(2, 0).start()
        hid_copy(2, 1).start()
        win_copy(1).start()

    win_copy(0).start()

    @pl.when(near)
    def _():
        hid[core, tok] = mine[...]
        win[core] = win_mine[...]

    def sub_rows(h, part):
        return pl.ds(pl.multiple_of((2 * h + part) * half, half), half)

    def kv_copy(kind, g, o, h, part, to_g, device):
        at = sub_rows(h, part)
        return remote(
            kv.at[g, o, :, at, :], kv.at[to_g, o, :, at, :],
            kv_send.at[kind, o, 2 * h + part], kv_recv.at[to_g, o, 2 * h + part], device,
        )

    def kv_wait(g, o, h, part):
        kv_copy(0, g, o, h, part, g, beside).wait_recv()

    def old_core(o):
        return jnp.where(o == 3, 1, 0)

    def own_next(o, h, part):
        return kv_copy(0, 2, o, h, part, 1, dev(line + 1, z, core))

    def own_back(o, h, part):
        return kv_copy(1, 2, o, h, part, 3, dev(back_line, z, core))

    def own_share(o, h, part):
        return kv_copy(2, 2, o, h, part, 2, beside)

    def pass_next(o, h, part):
        return kv_copy(3, 1, o, h, part, 0, dev(line + 1, z, old_core(o)))

    def pass_share(o, h, part):
        return kv_copy(4, 1, o, h, part, 1, beside)

    def pass_back(o, h, part):
        return kv_copy(5, 3, o, h, part, 0, dev(back_from + 2, z, old_core(o)))

    def old_share(h, part):
        return kv_copy(6, 0, 3, h, part, 0, beside)

    def sub_of(k):
        h = jnp.where(near, (tok + k // 4) % 2, k % 2)
        p = jnp.where(near, (core + k // 2) % 2, (k // 2) % 2)
        part = jnp.where(near, k % 2, (first_part(h) + k // 4) % 2)
        return p, h, part

    def by_next(k):
        return jnp.logical_and(k < 4, k % 2 == 0)

    def own_goes(k, o):
        return has_next, jnp.logical_and(jnp.logical_and(has_next2, o > 0), jnp.logical_not(by_next(k))), core == 0

    def pass_goes(k, o):
        return (
            jnp.logical_and(jnp.logical_and(has_prev, has_next), jnp.logical_and(o > 0, by_next(k))),
            jnp.logical_and(has_back, jnp.logical_and(o > 0, jnp.logical_not(by_next(k)))),
        )

    def head_norm(v, which, hd):
        scaled = v * lax.rsqrt(jnp.mean(v * v, axis=-1, keepdims=True) + EPSILON)
        at = pl.ds(pl.multiple_of(zlo * cols + hd * HEAD_DIM, 128), HEAD_DIM)
        return (scaled * gain[which:which + 1, at]).astype(jnp.bfloat16)

    def own_pair(kk, carry):
        subs = [sub_of(2 * kk), sub_of(2 * kk + 1)]
        p = subs[0][0]
        o = 2 * core + p
        for _, h, part in subs:
            @pl.when(jnp.logical_or(jnp.logical_not(near), kk > 0))
            def _():
                hid_wait(p, h, part)

                @pl.when(jnp.logical_and(jnp.logical_not(near), kk < 2))
                def _():
                    hid_pass(p, h).start()

        v = jnp.concatenate([hid[p, h, half_at(part), :] for _, h, part in subs], axis=0)
        keys = dot(v, w[1])
        values = dot(v, w[2])
        for hd in range(GROUP):
            lanes = slice(hd * HEAD_DIM, (hd + 1) * HEAD_DIM)
            normed = head_norm(keys[:, lanes], 1, hd)
            plain = values[:, lanes].astype(jnp.bfloat16)
            for n, (_, h, part) in enumerate(subs):
                kv[2, o, hd, sub_rows(h, part), :] = normed[n * half:(n + 1) * half]
                kv[2, o, GROUP + hd, sub_rows(h, part), :] = plain[n * half:(n + 1) * half]
        for n, (_, h, part) in enumerate(subs):
            for flag, copy in zip(own_goes(2 * kk + n, o), (own_next, own_back, own_share)):
                @pl.when(flag)
                def _():
                    copy(o, h, part).start()

        queries = dot(v, w[0])
        for hd in range(GROUP):
            lanes = slice(hd * HEAD_DIM, (hd + 1) * HEAD_DIM)
            normed = head_norm(queries[:, lanes], 0, hd)
            for n, (_, h, part) in enumerate(subs):
                q[p, hd, sub_rows(h, part), :] = normed[n * half:(n + 1) * half]
        return carry

    def pass_sub(k, carry):
        p, h, part = sub_of(k)
        o = 2 * core + p
        go_next, go_back = pass_goes(k, o)

        @pl.when(has_prev)
        def _():
            kv_wait(1, o, h, part)

            @pl.when(go_next)
            def _():
                pass_next(o, h, part).start()

            pass_share(o, h, part).start()

        @pl.when(go_back)
        def _():
            kv_wait(3, o, h, part)
            pass_back(o, h, part).start()

        return carry

    for c in (1, 2, 0):
        w_copy(c).wait()
    ow_copy().start()
    lax.fori_loop(0, 2, own_pair, 0)

    text_keys = dot(text[...], w[1])
    text_values = dot(text[...], w[2])
    for hd in range(GROUP):
        lanes = slice(hd * HEAD_DIM, (hd + 1) * HEAD_DIM)
        tk[hd] = head_norm(text_keys[:, lanes], 1, hd)
        tk[GROUP + hd] = text_values[:, lanes].astype(jnp.bfloat16)

    lax.fori_loop(0, 2, pass_sub, 0)
    hid_copy(0, 0).wait_send()
    hid_copy(1, 1).wait_send()
    hid_copy(0, 1).start()
    hid_copy(1, 0).start()
    lax.fori_loop(2, 4, pass_sub, 0)
    lax.fori_loop(2, 4, own_pair, 0)

    piece_rows = width // 2 // (2 * depth)

    def piece(n):
        return pl.ds(pl.multiple_of(n * piece_rows, 16), piece_rows)

    my_piece = 2 * y + core

    def ow_cross(which=None):
        of = tok if which is None else which
        return remote(
            ow.at[tok, piece(my_piece), :], ow.at[of, piece(my_piece), :],
            ow_send.at[0], ow_recv.at[my_piece], dev(line, 3 - z, core),
        )

    def ow_along(d):
        return remote(
            ow.at[1 - tok, piece(my_piece), :], ow.at[1 - tok, piece(my_piece), :],
            ow_send.at[d], ow_recv.at[my_piece], dev(4 * ((y + d) % depth) + x, z, core),
        )

    def ow_share(d, which):
        n = 2 * ((y + d) % depth) + which
        return remote(
            ow.at[1 - tok, piece(n), :], ow.at[1 - tok, piece(n), :],
            ow_send.at[depth + d], ow_recv.at[n], beside,
        )

    ow_copy().wait()
    ow_cross().start()

    @pl.when(near)
    def _():
        win_copy(0).wait_send()

    @pl.when(jnp.logical_not(near))
    def _():
        win_copy(0).wait_send()
        win_copy(1).wait_send()

    def win_wait(p):
        remote(win_mine, win.at[p], win_send.at[0], win_recv.at[p], beside).wait_recv()

    @pl.when(near)
    def _():
        win_wait(partner)

    @pl.when(jnp.logical_not(near))
    def _():
        win_wait(0)
        win_wait(1)

    def text_attend(t, carry):
        p, hd = t // GROUP, t % GROUP
        s = dot_t(q[p, hd], tk[hd])
        s = jnp.where(lax.broadcasted_iota(jnp.int32, s.shape, 1) < count[0], s, LOW)
        m = jnp.broadcast_to(jnp.max(s, axis=1, keepdims=True) * SCALE, (2 * rows, HEAD_DIM))
        e = [jnp.exp2(s[:, n:n + HEAD_DIM] * SCALE - m) for n in range(0, s.shape[1], HEAD_DIM)]
        top[p, hd] = m
        tot[p, hd] = functools.reduce(jnp.add, e)
        acc[p, hd] = dot(jnp.concatenate([v.astype(jnp.bfloat16) for v in e], axis=1), tk[GROUP + hd])
        return carry

    def frame_attend(g, o):
        frame = (4 * (line - 2) + 4 * g + o).astype(jnp.float32)

        def step(t, carry):
            p, hd = t // GROUP, t % GROUP
            inside = jnp.logical_and(frame >= win[p, 0, :1], frame < win[p, 1, :1])
            s = dot_t(q[p, hd], kv[g, o, hd])
            m = jnp.broadcast_to(jnp.max(s, axis=1, keepdims=True) * SCALE, (2 * rows, HEAD_DIM))
            before = top[p, hd]
            m = jnp.maximum(before, jnp.where(inside, m, LOW))
            top[p, hd] = m
            shrink = jnp.exp2(before - m)
            m = jnp.where(inside, m, -LOW)
            e = [jnp.exp2(s[:, n:n + HEAD_DIM] * SCALE - m) for n in range(0, s.shape[1], HEAD_DIM)]
            tot[p, hd] = tot[p, hd] * shrink + functools.reduce(jnp.add, e)
            acc[p, hd] = acc[p, hd] * shrink + dot(
                jnp.concatenate([v.astype(jnp.bfloat16) for v in e], axis=1), kv[g, o, GROUP + hd]
            )
            return carry

        return step

    lax.fori_loop(0, 2 * GROUP, text_attend, 0)
    pass_sub(4, 0)
    lax.fori_loop(0, GROUP, frame_attend(2, 2 * core), 0)
    pass_sub(5, 0)
    lax.fori_loop(GROUP, 2 * GROUP, frame_attend(2, 2 * core), 0)
    pass_sub(6, 0)
    lax.fori_loop(GROUP, 2 * GROUP, frame_attend(2, 2 * core + 1), 0)
    pass_sub(7, 0)

    def slot(j):
        s = 1 + 2 * core + j
        return s // 4, s % 4

    def slot_wait(g, o):
        for n in range(4):
            h, part = n // 2, n % 2
            kv_wait(g, o, h, part)

            @pl.when(jnp.logical_and(g == 0, core == 1))
            def _():
                old_share(h, part).start()

    def newer(i, carry):
        g, o = slot(6 - i)

        @pl.when(jnp.logical_and(g > 0, line + g >= 2))
        def _():
            @pl.when(jnp.logical_or(g != 1, o // 2 != core))
            def _():
                slot_wait(g, o)

            lax.fori_loop(0, 2 * GROUP, frame_attend(g, o), 0)

        return carry

    lax.fori_loop(0, 6, newer, 0)

    ow_cross(1 - tok).wait_recv()
    for d in range(1, depth):
        ow_along(d).start()
    ow_share(0, core).start()

    def att_copy(p, h):
        return remote(
            att.at[p, h], attin.at[z], att_send.at[p, h], att_recv.at[z], dev(line, 2 * h + core, p)
        )

    def is_here(p, h):
        return jnp.logical_and(2 * h + core == z, p == core)

    def finish(p):
        for hd in range(GROUP):
            lanes = slice(hd * HEAD_DIM, (hd + 1) * HEAD_DIM)
            total = jnp.sum(tot[p, hd], axis=1, keepdims=True)
            result = (acc[p, hd] / total).astype(jnp.bfloat16)
            for h in range(2):
                att[p, h, :, lanes] = result[h * rows:(h + 1) * rows]
        for h in range(2):
            here = is_here(p, h)

            @pl.when(jnp.logical_not(here))
            def _():
                att_copy(p, h).start()

            @pl.when(here)
            def _():
                attin[z] = att[p, h]

    for j in (2, 1):
        @pl.when(jnp.logical_and(line >= 2, core == 0))
        def _():
            g, o = 0, 1 + j
            slot_wait(g, o)
            lax.fori_loop(GROUP, 2 * GROUP, frame_attend(g, o), 0)

    finish(1)

    @pl.when(jnp.logical_and(line >= 2, core == 0))
    def _():
        slot_wait(0, 1)
        for o in (3, 2, 1):
            lax.fori_loop(0, GROUP, frame_attend(0, o), 0)

    @pl.when(jnp.logical_and(line >= 2, core == 1))
    def _():
        slot_wait(0, 3)
        lax.fori_loop(0, GROUP, frame_attend(0, 3), 0)

    finish(0)

    for d in range(1, depth):
        n = 2 * ((y + d) % depth) + core
        remote(
            ow.at[1 - tok, piece(n), :], ow.at[1 - tok, piece(n), :], ow_send.at[d], ow_recv.at[n], beside
        ).wait_recv()
        ow_share(d, core).start()
    for d in range(depth):
        ow_share(d, partner).wait_recv()

    for s in range(4):
        @pl.when(jnp.logical_not(jnp.logical_and(s == z, near)))
        def _():
            remote(att.at[0, 0], attin.at[s], att_send.at[0, 0], att_recv.at[s], beside).wait_recv()

    step_cols = 256

    def project(n, carry):
        at = pl.ds(pl.multiple_of(n * step_cols, step_cols), step_cols)
        update = dot(attin[0], ow[0, :cols, at])
        update += dot(attin[1], ow[0, cols:, at])
        update += dot(attin[2], ow[1, :cols, at])
        update += dot(attin[3], ow[1, cols:, at])
        out[:, at] = (tokens[:, at].astype(jnp.float32) + mod[0, 2:3, at] * update).astype(jnp.bfloat16)
        return carry

    lax.fori_loop(0, width // step_cols, project, 0)

    hid_copy(0, 1).wait_send()
    hid_copy(1, 0).wait_send()

    @pl.when(jnp.logical_not(near))
    def _():
        hid_copy(2, 0).wait_send()
        hid_copy(2, 1).wait_send()
        for p in range(2):
            for h in range(2):
                hid_pass(p, h).wait_send()

    ow_cross().wait_send()
    for d in range(1, depth):
        ow_along(d).wait_send()
    for d in range(depth):
        ow_share(d, core).wait_send()

    for p in range(2):
        for h in range(2):
            @pl.when(jnp.logical_not(is_here(p, h)))
            def _():
                att_copy(p, h).wait_send()

    def drain(k, carry):
        p, h, part = sub_of(k)
        o = 2 * core + p
        for flag, copy in zip(own_goes(k, o), (own_next, own_back, own_share)):
            @pl.when(flag)
            def _():
                copy(o, h, part).wait_send()

        for flag, copy in zip(pass_goes(k, o), (pass_next, pass_back)):
            @pl.when(flag)
            def _():
                copy(o, h, part).wait_send()

        @pl.when(has_prev)
        def _():
            pass_share(o, h, part).wait_send()

        @pl.when(jnp.logical_and(jnp.logical_and(line >= 2, core == 1), p == 0))
        def _():
            old_share(h, part).wait_send()

        return carry

    lax.fori_loop(0, 8, drain, 0)


def shards(groups, tokens, modulation, qkv_weight, out_weight, qk_gain, text, text_count, window):
    rows, width = tokens.shape
    text_rows = text.shape[0]
    cols = GROUP * HEAD_DIM
    depth = max(groups // 4, 1)
    bf16, f32 = jnp.bfloat16, jnp.float32
    vmem = pl.BlockSpec(memory_space=pltpu.VMEM)
    smem = pl.BlockSpec(memory_space=pltpu.SMEM)
    hbm = pl.BlockSpec(memory_space=pl.ANY)
    dma = pltpu.SemaphoreType.DMA
    return pl.pallas_call(
        functools.partial(kernel, groups),
        out_shape=jax.ShapeDtypeStruct((rows, width), bf16),
        in_specs=[vmem, vmem, hbm, hbm, vmem, vmem, smem, smem],
        out_specs=vmem,
        scratch_shapes=[
            pltpu.VMEM((rows, width), bf16),
            pltpu.VMEM((2, 2, rows, width), bf16),
            pltpu.VMEM((2, 8, HEAD_DIM), f32),
            pltpu.VMEM((2, 2, 8, HEAD_DIM), f32),
            pltpu.VMEM((3, width, cols), bf16),
            pltpu.VMEM((2, width // 2, width), bf16),
            pltpu.VMEM((4, 4, 2 * GROUP, 2 * rows, HEAD_DIM), bf16),
            pltpu.VMEM((2 * GROUP, text_rows, HEAD_DIM), bf16),
            pltpu.VMEM((2, GROUP, 2 * rows, HEAD_DIM), bf16),
            pltpu.VMEM((2, GROUP, 2 * rows, HEAD_DIM), f32),
            pltpu.VMEM((2, GROUP, 2 * rows, HEAD_DIM), f32),
            pltpu.VMEM((2, GROUP, 2 * rows, HEAD_DIM), f32),
            pltpu.VMEM((2, 2, rows, cols), bf16),
            pltpu.VMEM((4, rows, cols), bf16),
            dma((4,)),
            dma((3, 2)),
            dma((2, 2)),
            dma((2, 2, 2)),
            dma((2,)),
            dma((2,)),
            dma((7, 4, 4)),
            dma((4, 4, 4)),
            dma((2 * depth,)),
            dma((2 * depth,)),
            dma((2, 2)),
            dma((4,)),
        ],
        compiler_params=pltpu.CompilerParams(
            collective_id=0, has_side_effects=True, vmem_limit_bytes=58 * 1024 * 1024
        ),
        cost_estimate=pl.CostEstimate(flops=13_000_000_000, bytes_accessed=12_000_000, transcendentals=13_400_000),
    )(tokens, modulation, qkv_weight, out_weight, qk_gain, text, text_count, window)


def solution(mesh):
    in_specs = (
        P(("frame", "tok"), None),
        P("frame", None, None),
        P(None, None, "tok"),
        P("tok", None),
        P(None, "tok"),
        P(),
        P(),
        P("frame", None),
    )
    out_specs = P(("frame", "tok"), None)
    return jax.shard_map(
        functools.partial(shards, mesh.shape["frame"] // 4),
        mesh=mesh, in_specs=in_specs, out_specs=out_specs, check_vma=False,
    )
```

```python
import functools

import jax
import jax.numpy as jnp
from jax import lax
from jax.experimental import pallas as pl
from jax.experimental.pallas import tpu as pltpu
from jax.sharding import PartitionSpec as P

HEAD_DIM = 128
GROUP = 3
EPSILON = 1e-06
LOW = -1e30
SCALE = HEAD_DIM ** (-0.5) * 1.4426950408889634
MESH = pl.DeviceIdType.MESH


def dot(a, b):
    return jnp.dot(a, b, preferred_element_type=jnp.float32)


def dot_t(a, b):
    return lax.dot_general(a, b, (((1,), (1,)), ((), ())), preferred_element_type=jnp.float32)


def kernel(
    groups,
    tokens, mod, w_hbm, ow_hbm, gain, text, count, window,
    out,
    mine, hid, win_mine, win, w, ow, kv, tk, q, acc, top, tot, att, attin,
    w_sem, hid_send, hid_relay, hid_recv, win_send, win_recv, kv_send, kv_recv, ow_send, ow_recv, att_send, att_recv,
):
    rows, width = tokens.shape
    half = rows // 2
    cols = GROUP * HEAD_DIM
    depth = max(groups // 4, 1)
    fi = lax.axis_index("frame")
    tok = lax.axis_index("tok")
    line = fi // 4
    x = line % 4
    y = line // 4
    zlo = (fi // 2) % 2
    core = fi % 2
    z = 2 * tok + zlo
    partner = 1 - core
    near = core == zlo

    def dev(line_, z_, core_):
        return (4 * line_ + 2 * (z_ % 2) + core_, z_ // 2)

    def remote(src, dst, send, recv, device):
        return pltpu.make_async_remote_copy(
            src_ref=src, dst_ref=dst, send_sem=send, recv_sem=recv, device_id=device, device_id_type=MESH
        )

    beside = dev(line, z, partner)
    has_prev = line > 0
    has_next = line < groups - 1
    has_next2 = line < groups - 2
    back_line = jnp.where(x == 1, line - 1, line + 3)
    back_from = jnp.where(x == 0, line + 1, line - 3)
    has_back = jnp.logical_and(back_from >= 0, back_from < groups - 2)

    def w_copy(c):
        return pltpu.make_async_copy(
            w_hbm.at[c, :, pl.ds(pl.multiple_of(zlo * cols, 128), cols)], w.at[c], w_sem.at[c]
        )

    def ow_copy():
        return pltpu.make_async_copy(ow_hbm, ow.at[tok], w_sem.at[3])

    for c in (1, 2, 0):
        w_copy(c).start()

    barrier = pltpu.get_barrier_semaphore()

    def greet(device):
        pl.semaphore_signal(barrier, inc=1, device_id=device, device_id_type=MESH)

    for c in range(2):
        for d in range(1, 4):
            greet(dev(line, (z + d) % 4, c))
    greet(beside)

    for d in range(1, depth):
        greet(dev(4 * ((y + d) % depth) + x, z, core))

    def greet_line(line_):
        for c in range(2):
            greet(dev(line_, z, c))

    @pl.when(has_prev)
    def _():
        greet_line(line - 1)

    @pl.when(has_next)
    def _():
        greet_line(line + 1)

    @pl.when(has_next2)
    def _():
        greet(dev(back_line, z, core))

    @pl.when(has_back)
    def _():
        greet(dev(back_from, z, core))
        greet_line(back_from + 2)

    old_x = (line + 2) % 4
    old_relay = jnp.where(old_x == 1, line - 3, line + 1)

    @pl.when(line >= 2)
    def _():
        greet_line(old_relay)

    def ones(flag, n):
        return jnp.where(flag, n, 0)

    greeted = (
        7 + depth - 1 + ones(has_prev, 2) + ones(has_next, 2) + ones(has_next2, 1) + ones(has_back, 3) + ones(line >= 2, 2)
    )

    step_rows = 32

    def norm_rows(step, carry):
        at = pl.ds(pl.multiple_of(step * step_rows, step_rows), step_rows)
        v = tokens[at, :].astype(jnp.float32)
        v = v - jnp.mean(v, axis=-1, keepdims=True)
        spread = jnp.mean(v * v, axis=-1, keepdims=True)
        v = v * lax.rsqrt(spread + EPSILON)
        mine[at, :] = (v * (1.0 + mod[0, 1:2, :]) + mod[0, 0:1, :]).astype(jnp.bfloat16)
        return carry

    lax.fori_loop(0, rows // step_rows, norm_rows, 0)
    for n in range(2):
        win_mine[n] = jnp.full((8, HEAD_DIM), window[0, n], jnp.int32).astype(jnp.float32)

    pl.semaphore_wait(barrier, greeted)

    def half_at(part):
        return pl.ds(pl.multiple_of(part * half, half), half)

    def hid_copy(which, part):
        device = (dev(line, (z + 1) % 4, zlo), dev(line, (z + 3) % 4, zlo), dev(line, z, zlo))[which]
        return remote(
            mine.at[half_at(part), :], hid.at[core, tok, half_at(part), :],
            hid_send.at[which, part], hid_recv.at[core, tok, part], device,
        )

    def win_copy(which):
        device = (dev(line, (z + 1) % 4, zlo), dev(line, z, zlo))[which]
        return remote(win_mine, win.at[core], win_send.at[which], win_recv.at[core], device)

    def hid_wait(p, h, part):
        remote(
            mine.at[half_at(part), :], hid.at[p, h, half_at(part), :],
            hid_send.at[0, part], hid_recv.at[p, h, part], beside,
        ).wait_recv()

    def first_part(h):
        return jnp.where((2 * h + core + 1) % 4 == z, 0, 1)

    def hid_pass(p, h):
        part = first_part(h)
        return remote(
            hid.at[p, h, half_at(part), :], hid.at[p, h, half_at(part), :],
            hid_relay.at[p, h], hid_recv.at[p, h, part], dev(line, (z + 1 + 2 * part) % 4, core),
        )

    hid_copy(0, 0).start()
    hid_copy(1, 1).start()

    @pl.when(jnp.logical_not(near))
    def _():
        hid_copy(2, 0).start()
        hid_copy(2, 1).start()
        win_copy(1).start()

    win_copy(0).start()

    @pl.when(near)
    def _():
        hid[core, tok] = mine[...]
        win[core] = win_mine[...]

    def sub_rows(h, part):
        return pl.ds(pl.multiple_of((2 * h + part) * half, half), half)

    def kv_copy(kind, g, o, h, part, to_g, device):
        at = sub_rows(h, part)
        return remote(
            kv.at[g, o, :, at, :], kv.at[to_g, o, :, at, :],
            kv_send.at[kind, o, 2 * h + part], kv_recv.at[to_g, o, 2 * h + part], device,
        )

    def kv_wait(g, o, h, part):
        kv_copy(0, g, o, h, part, g, beside).wait_recv()

    def old_core(o):
        return jnp.where(o == 3, 1, 0)

    def own_next(o, h, part):
        return kv_copy(0, 2, o, h, part, 1, dev(line + 1, z, core))

    def own_back(o, h, part):
        return kv_copy(1, 2, o, h, part, 3, dev(back_line, z, core))

    def own_share(o, h, part):
        return kv_copy(2, 2, o, h, part, 2, beside)

    def pass_next(o, h, part):
        return kv_copy(3, 1, o, h, part, 0, dev(line + 1, z, old_core(o)))

    def pass_share(o, h, part):
        return kv_copy(4, 1, o, h, part, 1, beside)

    def pass_back(o, h, part):
        return kv_copy(5, 3, o, h, part, 0, dev(back_from + 2, z, old_core(o)))

    def old_share(h, part):
        return kv_copy(6, 0, 3, h, part, 0, beside)

    def sub_of(k):
        h = jnp.where(near, (tok + k // 4) % 2, k % 2)
        p = jnp.where(near, (core + k // 2) % 2, (k // 2) % 2)
        part = jnp.where(near, k % 2, (first_part(h) + k // 4) % 2)
        return p, h, part

    def by_next(k):
        return jnp.logical_and(k >= 4, k % 2 == 0)

    def own_goes(k, o):
        return has_next, jnp.logical_and(jnp.logical_and(has_next2, o > 0), jnp.logical_not(by_next(k))), core == 0

    def pass_goes(k, o):
        return (
            jnp.logical_and(jnp.logical_and(has_prev, has_next), jnp.logical_and(o > 0, by_next(k))),
            jnp.logical_and(has_back, jnp.logical_and(o > 0, jnp.logical_not(by_next(k)))),
        )

    def head_norm(v, which, hd):
        scaled = v * lax.rsqrt(jnp.mean(v * v, axis=-1, keepdims=True) + EPSILON)
        at = pl.ds(pl.multiple_of(zlo * cols + hd * HEAD_DIM, 128), HEAD_DIM)
        return (scaled * gain[which:which + 1, at]).astype(jnp.bfloat16)

    def own_pair(kk, carry):
        subs = [sub_of(2 * kk), sub_of(2 * kk + 1)]
        p = subs[0][0]
        o = 2 * core + p
        for _, h, part in subs:
            @pl.when(jnp.logical_or(jnp.logical_not(near), kk == 1))
            def _():
                hid_wait(p, h, part)

                @pl.when(jnp.logical_and(jnp.logical_not(near), kk < 2))
                def _():
                    hid_pass(p, h).start()

        v = jnp.concatenate([hid[p, h, half_at(part), :] for _, h, part in subs], axis=0)
        keys = dot(v, w[1])
        values = dot(v, w[2])
        for hd in range(GROUP):
            lanes = slice(hd * HEAD_DIM, (hd + 1) * HEAD_DIM)
            normed = head_norm(keys[:, lanes], 1, hd)
            plain = values[:, lanes].astype(jnp.bfloat16)
            for n, (_, h, part) in enumerate(subs):
                kv[2, o, hd, sub_rows(h, part), :] = normed[n * half:(n + 1) * half]
                kv[2, o, GROUP + hd, sub_rows(h, part), :] = plain[n * half:(n + 1) * half]
        for n, (_, h, part) in enumerate(subs):
            for flag, copy in zip(own_goes(2 * kk + n, o), (own_next, own_back, own_share)):
                @pl.when(flag)
                def _():
                    copy(o, h, part).start()

        queries = dot(v, w[0])
        for hd in range(GROUP):
            lanes = slice(hd * HEAD_DIM, (hd + 1) * HEAD_DIM)
            normed = head_norm(queries[:, lanes], 0, hd)
            for n, (_, h, part) in enumerate(subs):
                q[hd, sub_rows(2 * p + h, part), :] = normed[n * half:(n + 1) * half]
        return carry

    def pass_sub(k, carry):
        p, h, part = sub_of(k)
        o = 2 * core + p
        go_next, go_back = pass_goes(k, o)

        @pl.when(has_prev)
        def _():
            kv_wait(1, o, h, part)

            @pl.when(go_next)
            def _():
                pass_next(o, h, part).start()

            pass_share(o, h, part).start()

        @pl.when(go_back)
        def _():
            kv_wait(3, o, h, part)
            pass_back(o, h, part).start()

        return carry

    for c in (1, 2, 0):
        w_copy(c).wait()
    ow_copy().start()
    lax.fori_loop(0, 2, own_pair, 0)

    text_keys = dot(text[...], w[1])
    text_values = dot(text[...], w[2])
    for hd in range(GROUP):
        lanes = slice(hd * HEAD_DIM, (hd + 1) * HEAD_DIM)
        tk[hd] = head_norm(text_keys[:, lanes], 1, hd)
        tk[GROUP + hd] = text_values[:, lanes].astype(jnp.bfloat16)

    lax.fori_loop(0, 4, pass_sub, 0)

    @pl.when(jnp.logical_not(near))
    def _():
        for p in range(2):
            for h in range(2):
                hid_pass(p, h).wait_send()

    @pl.when(near)
    def _():
        for k in range(4, 8):
            hid_wait(*sub_of(k))

    hid_copy(0, 0).wait_send()
    hid_copy(1, 1).wait_send()
    hid_copy(0, 1).start()
    hid_copy(1, 0).start()
    lax.fori_loop(2, 4, own_pair, 0)

    piece_rows = width // 2 // (2 * depth)

    def piece(n):
        return pl.ds(pl.multiple_of(n * piece_rows, 16), piece_rows)

    my_piece = 2 * y + core

    def ow_cross(which=None):
        of = tok if which is None else which
        return remote(
            ow.at[tok, piece(my_piece), :], ow.at[of, piece(my_piece), :],
            ow_send.at[0], ow_recv.at[my_piece], dev(line, 3 - z, core),
        )

    def ow_along(d):
        return remote(
            ow.at[1 - tok, piece(my_piece), :], ow.at[1 - tok, piece(my_piece), :],
            ow_send.at[d], ow_recv.at[my_piece], dev(4 * ((y + d) % depth) + x, z, core),
        )

    def ow_share(d, which):
        n = 2 * ((y + d) % depth) + which
        return remote(
            ow.at[1 - tok, piece(n), :], ow.at[1 - tok, piece(n), :],
            ow_send.at[depth + d], ow_recv.at[n], beside,
        )


    @pl.when(near)
    def _():
        win_copy(0).wait_send()

    @pl.when(jnp.logical_not(near))
    def _():
        win_copy(0).wait_send()
        win_copy(1).wait_send()

    def win_wait(p):
        remote(win_mine, win.at[p], win_send.at[0], win_recv.at[p], beside).wait_recv()

    @pl.when(near)
    def _():
        win_wait(partner)

    @pl.when(jnp.logical_not(near))
    def _():
        win_wait(0)
        win_wait(1)

    def attend(keys, values, spans, text_keys=False):
        first, size = spans[0][0] * 2 * rows, 2 * rows
        at = slice(first, first + len(spans) * size)
        for hd in range(GROUP):
            s = dot_t(q[hd, at, :], keys(hd))
            if text_keys:
                s = jnp.where(lax.broadcasted_iota(jnp.int32, s.shape, 1) < count[0], s, LOW)
            weights, shrinks = [], []
            for n, (p, low) in enumerate(spans):
                mine_at = slice(p * size, (p + 1) * size)
                part = s[n * size:(n + 1) * size]
                m = jnp.broadcast_to(jnp.max(part, axis=1, keepdims=True) * SCALE, (size, HEAD_DIM))
                if not text_keys:
                    before = top[hd, mine_at, :]
                    m = jnp.maximum(before, m + low)
                    shrink = jnp.exp2(before - m)
                    shrinks.append(shrink)
                top[hd, mine_at, :] = m
                if not text_keys:
                    m = m - low
                e = [jnp.exp2(part[:, c:c + HEAD_DIM] * SCALE - m) for c in range(0, s.shape[1], HEAD_DIM)]
                total = functools.reduce(jnp.add, e)
                tot[hd, mine_at, :] = total if text_keys else tot[hd, mine_at, :] * shrink + total
                weights.append(jnp.concatenate([v.astype(jnp.bfloat16) for v in e], axis=1))
            summed = dot(jnp.concatenate(weights, axis=0), values(hd))
            acc[hd, at, :] = summed if text_keys else acc[hd, at, :] * jnp.concatenate(shrinks, axis=0) + summed

    def text_attend():
        attend(lambda hd: tk[hd], lambda hd: tk[GROUP + hd], [(0, 0.0), (1, 0.0)], text_keys=True)

    def frame_attend(g, o, ps=(0, 1)):
        frame = (4 * (line - 2) + 4 * g + o).astype(jnp.float32)

        def low(p):
            inside = jnp.logical_and(frame >= win[p, 0, :1], frame < win[p, 1, :1])
            return jnp.where(inside, 0.0, LOW)

        attend(lambda hd: kv[g, o, hd], lambda hd: kv[g, o, GROUP + hd], [(p, low(p)) for p in ps])

    text_attend()
    lax.fori_loop(4, 6, pass_sub, 0)
    frame_attend(2, 2 * core)
    pass_sub(6, 0)
    frame_attend(2, 2 * core + 1, (1,))
    pass_sub(7, 0)
    ow_copy().wait()
    ow_cross().start()

    def slot_wait(g, o):
        for n in range(4):
            h, part = n // 2, n % 2
            kv_wait(g, o, h, part)

            @pl.when(jnp.logical_and(g == 0, core == 1))
            def _():
                old_share(h, part).start()

    def newer(i, carry):
        kind = jnp.where(near, i // 2, (i // 2 + 1) % 3)
        g = jnp.where(kind == 1, 2, 1)
        o = 2 * jnp.where(kind == 0, core, partner) + 1 - i % 2

        @pl.when(jnp.where(kind == 1, core == 1, has_prev))
        def _():
            @pl.when(kind != 0)
            def _():
                slot_wait(g, o)

            frame_attend(g, o)

        return carry

    lax.fori_loop(0, 6, newer, 0)

    ow_cross(1 - tok).wait_recv()
    for d in range(1, depth):
        ow_along(d).start()
    ow_share(0, core).start()

    def att_copy(p, h):
        return remote(
            att.at[p, h], attin.at[z], att_send.at[p, h], att_recv.at[z], dev(line, 2 * h + core, p)
        )

    def is_here(p, h):
        return jnp.logical_and(2 * h + core == z, p == core)

    def finish(p):
        for hd in range(GROUP):
            lanes = slice(hd * HEAD_DIM, (hd + 1) * HEAD_DIM)
            at = slice(p * 2 * rows, (p + 1) * 2 * rows)
            total = jnp.sum(tot[hd, at, :], axis=1, keepdims=True)
            result = (acc[hd, at, :] / total).astype(jnp.bfloat16)
            for h in range(2):
                att[p, h, :, lanes] = result[h * rows:(h + 1) * rows]
        for h in range(2):
            here = is_here(p, h)

            @pl.when(jnp.logical_not(here))
            def _():
                att_copy(p, h).start()

            @pl.when(here)
            def _():
                attin[z] = att[p, h]

    @pl.when(jnp.logical_and(line >= 2, core == 0))
    def _():
        def oldest(n, carry):
            slot_wait(0, 3 - n)
            frame_attend(0, 3 - n)
            return carry

        lax.fori_loop(0, 2, oldest, 0)

    finish(1)

    @pl.when(line >= 2)
    def _():
        o = jnp.where(core == 0, 1, 3)
        slot_wait(0, o)
        frame_attend(0, o, (0,))

    finish(0)

    for d in range(1, depth):
        n = 2 * ((y + d) % depth) + core
        remote(
            ow.at[1 - tok, piece(n), :], ow.at[1 - tok, piece(n), :], ow_send.at[d], ow_recv.at[n], beside
        ).wait_recv()
        ow_share(d, core).start()
    for d in range(depth):
        ow_share(d, partner).wait_recv()

    for s in range(4):
        @pl.when(jnp.logical_not(jnp.logical_and(s == z, near)))
        def _():
            remote(att.at[0, 0], attin.at[s], att_send.at[0, 0], att_recv.at[s], beside).wait_recv()

    step_cols = 256

    def project(n, carry):
        at = pl.ds(pl.multiple_of(n * step_cols, step_cols), step_cols)
        update = dot(attin[0], ow[0, :cols, at])
        update += dot(attin[1], ow[0, cols:, at])
        update += dot(attin[2], ow[1, :cols, at])
        update += dot(attin[3], ow[1, cols:, at])
        out[:, at] = (tokens[:, at].astype(jnp.float32) + mod[0, 2:3, at] * update).astype(jnp.bfloat16)
        return carry

    lax.fori_loop(0, width // step_cols, project, 0)

    hid_copy(0, 1).wait_send()
    hid_copy(1, 0).wait_send()

    @pl.when(jnp.logical_not(near))
    def _():
        hid_copy(2, 0).wait_send()
        hid_copy(2, 1).wait_send()

    ow_cross().wait_send()
    for d in range(1, depth):
        ow_along(d).wait_send()
    for d in range(depth):
        ow_share(d, core).wait_send()

    for p in range(2):
        for h in range(2):
            @pl.when(jnp.logical_not(is_here(p, h)))
            def _():
                att_copy(p, h).wait_send()

    def drain(k, carry):
        p, h, part = sub_of(k)
        o = 2 * core + p
        for flag, copy in zip(own_goes(k, o), (own_next, own_back, own_share)):
            @pl.when(flag)
            def _():
                copy(o, h, part).wait_send()

        for flag, copy in zip(pass_goes(k, o), (pass_next, pass_back)):
            @pl.when(flag)
            def _():
                copy(o, h, part).wait_send()

        @pl.when(has_prev)
        def _():
            pass_share(o, h, part).wait_send()

        @pl.when(jnp.logical_and(jnp.logical_and(line >= 2, core == 1), p == 0))
        def _():
            old_share(h, part).wait_send()

        return carry

    lax.fori_loop(0, 8, drain, 0)


def shards(groups, tokens, modulation, qkv_weight, out_weight, qk_gain, text, text_count, window):
    rows, width = tokens.shape
    text_rows = text.shape[0]
    cols = GROUP * HEAD_DIM
    depth = max(groups // 4, 1)
    bf16, f32 = jnp.bfloat16, jnp.float32
    vmem = pl.BlockSpec(memory_space=pltpu.VMEM)
    smem = pl.BlockSpec(memory_space=pltpu.SMEM)
    hbm = pl.BlockSpec(memory_space=pl.ANY)
    dma = pltpu.SemaphoreType.DMA
    return pl.pallas_call(
        functools.partial(kernel, groups),
        out_shape=jax.ShapeDtypeStruct((rows, width), bf16),
        in_specs=[vmem, vmem, hbm, hbm, vmem, vmem, smem, smem],
        out_specs=vmem,
        scratch_shapes=[
            pltpu.VMEM((rows, width), bf16),
            pltpu.VMEM((2, 2, rows, width), bf16),
            pltpu.VMEM((2, 8, HEAD_DIM), f32),
            pltpu.VMEM((2, 2, 8, HEAD_DIM), f32),
            pltpu.VMEM((3, width, cols), bf16),
            pltpu.VMEM((2, width // 2, width), bf16),
            pltpu.VMEM((4, 4, 2 * GROUP, 2 * rows, HEAD_DIM), bf16),
            pltpu.VMEM((2 * GROUP, text_rows, HEAD_DIM), bf16),
            pltpu.VMEM((GROUP, 4 * rows, HEAD_DIM), bf16),
            pltpu.VMEM((GROUP, 4 * rows, HEAD_DIM), f32),
            pltpu.VMEM((GROUP, 4 * rows, HEAD_DIM), f32),
            pltpu.VMEM((GROUP, 4 * rows, HEAD_DIM), f32),
            pltpu.VMEM((2, 2, rows, cols), bf16),
            pltpu.VMEM((4, rows, cols), bf16),
            dma((4,)),
            dma((3, 2)),
            dma((2, 2)),
            dma((2, 2, 2)),
            dma((2,)),
            dma((2,)),
            dma((7, 4, 4)),
            dma((4, 4, 4)),
            dma((2 * depth,)),
            dma((2 * depth,)),
            dma((2, 2)),
            dma((4,)),
        ],
        compiler_params=pltpu.CompilerParams(
            collective_id=0, has_side_effects=True, vmem_limit_bytes=58 * 1024 * 1024
        ),
        cost_estimate=pl.CostEstimate(flops=13_000_000_000, bytes_accessed=12_000_000, transcendentals=13_400_000),
    )(tokens, modulation, qkv_weight, out_weight, qk_gain, text, text_count, window)


def solution(mesh):
    in_specs = (
        P(("frame", "tok"), None),
        P("frame", None, None),
        P(None, None, "tok"),
        P("tok", None),
        P(None, "tok"),
        P(),
        P(),
        P("frame", None),
    )
    out_specs = P(("frame", "tok"), None)
    return jax.shard_map(
        functools.partial(shards, mesh.shape["frame"] // 4),
        mesh=mesh, in_specs=in_specs, out_specs=out_specs, check_vma=False,
    )
```

```python
import functools

import jax
import jax.numpy as jnp
from jax import lax
from jax.experimental import pallas as pl
from jax.experimental.pallas import tpu as pltpu
from jax.sharding import PartitionSpec as P

HEAD_DIM = 128
GROUP = 3
EPSILON = 1e-06
LOW = -1e30
SCALE = HEAD_DIM ** (-0.5) * 1.4426950408889634
MESH = pl.DeviceIdType.MESH


def dot(a, b):
    return jnp.dot(a, b, preferred_element_type=jnp.float32)


def dot_t(a, b):
    return lax.dot_general(a, b, (((1,), (1,)), ((), ())), preferred_element_type=jnp.float32)


def kernel(
    groups,
    tokens, mod, w_hbm, ow_hbm, gain, text, count, window,
    out,
    hid, win_mine, win, w, ow, kv, tk, q, acc, top, tot, att, attin,
    w_sem, hid_send, hid_relay, hid_recv, win_send, win_recv, kv_send, kv_recv, ow_send, ow_recv, att_send, att_recv,
):
    rows, width = tokens.shape
    half = rows // 2
    cols = GROUP * HEAD_DIM
    depth = max(groups // 4, 1)
    fi = lax.axis_index("frame")
    tok = lax.axis_index("tok")
    line = fi // 4
    x = line % 4
    y = line // 4
    zlo = (fi // 2) % 2
    core = fi % 2
    z = 2 * tok + zlo
    partner = 1 - core
    a_late, a_soon = zlo, 1 - zlo

    def dev(line_, z_, core_):
        return (4 * line_ + 2 * (z_ % 2) + core_, z_ // 2)

    def remote(src, dst, send, recv, device):
        return pltpu.make_async_remote_copy(
            src_ref=src, dst_ref=dst, send_sem=send, recv_sem=recv, device_id=device, device_id_type=MESH
        )

    beside = dev(line, z, partner)
    has_prev = line > 0
    has_next = line < groups - 1
    has_next2 = line < groups - 2
    back_line = jnp.where(x == 1, line - 1, line + 3)
    back_from = jnp.where(x == 0, line + 1, line - 3)
    has_back = jnp.logical_and(back_from >= 0, back_from < groups - 2)

    def w_copy(c):
        return pltpu.make_async_copy(
            w_hbm.at[c, :, pl.ds(pl.multiple_of(zlo * cols, 128), cols)], w.at[c], w_sem.at[c]
        )

    def ow_copy():
        return pltpu.make_async_copy(ow_hbm, ow.at[tok], w_sem.at[3])

    for c in (1, 2, 0):
        w_copy(c).start()

    barrier = pltpu.get_barrier_semaphore()

    def greet(device):
        pl.semaphore_signal(barrier, inc=1, device_id=device, device_id_type=MESH)

    for c in range(2):
        for d in range(1, 4):
            greet(dev(line, (z + d) % 4, c))
    greet(beside)

    for d in range(1, depth):
        greet(dev(4 * ((y + d) % depth) + x, z, core))

    def greet_line(line_):
        for c in range(2):
            greet(dev(line_, z, c))

    @pl.when(has_prev)
    def _():
        greet_line(line - 1)

    @pl.when(has_next)
    def _():
        greet_line(line + 1)

    @pl.when(has_next2)
    def _():
        greet(dev(back_line, z, core))

    @pl.when(has_back)
    def _():
        greet(dev(back_from, z, core))
        greet_line(back_from + 2)

    old_x = (line + 2) % 4
    old_relay = jnp.where(old_x == 1, line - 3, line + 1)

    @pl.when(line >= 2)
    def _():
        greet_line(old_relay)

    def ones(flag, n):
        return jnp.where(flag, n, 0)

    greeted = (
        7 + depth - 1 + ones(has_prev, 2) + ones(has_next, 2) + ones(has_next2, 1) + ones(has_back, 3) + ones(line >= 2, 2)
    )

    step_rows = 32

    def norm_rows(step, carry):
        at = pl.ds(pl.multiple_of(step * step_rows, step_rows), step_rows)
        v = tokens[at, :].astype(jnp.float32)
        v = v - jnp.mean(v, axis=-1, keepdims=True)
        spread = jnp.mean(v * v, axis=-1, keepdims=True)
        v = v * lax.rsqrt(spread + EPSILON)
        hid[zlo, tok, at, :] = (v * (1.0 + mod[0, 1:2, :]) + mod[0, 0:1, :]).astype(jnp.bfloat16)
        return carry

    lax.fori_loop(0, rows // step_rows, norm_rows, 0)
    for n in range(2):
        win_mine[n] = jnp.full((8, HEAD_DIM), window[0, n], jnp.int32).astype(jnp.float32)

    pl.semaphore_wait(barrier, greeted)

    def half_at(part):
        return pl.ds(pl.multiple_of(part * half, half), half)

    half_below = ((z + 3) % 4) // 2
    half_above = ((z + 1) % 4) // 2

    def hid_copy(up, part):
        at = half_at(part)
        return remote(
            hid.at[zlo, tok, at, :], hid.at[zlo, tok, at, :],
            hid_send.at[up, part], hid_recv.at[zlo, tok, part], dev(line, (z + (1 if up else 3)) % 4, core),
        )

    win_copy = remote(win_mine, win.at[zlo], win_send, win_recv, dev(line, (z + 1) % 4, core))

    def hid_wait(a, h, part):
        at = half_at(part)
        remote(
            hid.at[a, h, at, :], hid.at[a, h, at, :], hid_send.at[0, part], hid_recv.at[a, h, part], beside
        ).wait_recv()

    def hid_pass(up):
        h, part = (half_below, 0) if up else (half_above, 1)
        at = half_at(part)
        return remote(
            hid.at[a_soon, h, at, :], hid.at[a_soon, h, at, :],
            hid_relay.at[up], hid_recv.at[a_soon, h, part], dev(line, (z + (1 if up else 3)) % 4, core),
        )

    hid_copy(1, 0).start()
    hid_copy(0, 1).start()
    hid_copy(1, 1).start()
    hid_copy(0, 0).start()
    win_copy.start()
    win[zlo] = win_mine[...]

    def sub_rows(h, part):
        return pl.ds(pl.multiple_of((2 * h + part) * half, half), half)

    def kv_copy(kind, g, o, h, part, to_g, device):
        at = sub_rows(h, part)
        return remote(
            kv.at[g, o, :, at, :], kv.at[to_g, o, :, at, :],
            kv_send.at[kind, o, 2 * h + part], kv_recv.at[to_g, o, 2 * h + part], device,
        )

    def kv_wait(g, o, h, part):
        kv_copy(0, g, o, h, part, g, beside).wait_recv()

    def old_core(o):
        return jnp.where(o == 3, 1, 0)

    def own_next(o, h, part):
        return kv_copy(0, 2, o, h, part, 1, dev(line + 1, z, core))

    def own_back(o, h, part):
        return kv_copy(1, 2, o, h, part, 3, dev(back_line, z, core))

    def own_share(o, h, part):
        return kv_copy(2, 2, o, h, part, 2, beside)

    def pass_next(o, h, part):
        return kv_copy(3, 1, o, h, part, 0, dev(line + 1, z, old_core(o)))

    def pass_share(o, h, part):
        return kv_copy(4, 1, o, h, part, 1, beside)

    def pass_back(o, h, part):
        return kv_copy(5, 3, o, h, part, 0, dev(back_from + 2, z, old_core(o)))

    def old_share(h, part):
        return kv_copy(6, 0, 2 + core, h, part, 0, beside)

    def sub_of(k):
        kk, e = k // 2, k % 2
        outer = jnp.logical_or(kk == 0, kk == 3)
        a = jnp.where(outer, a_late, a_soon)
        h = jnp.where(outer, (tok + kk // 3) % 2, jnp.where(e == 0, half_below, half_above))
        part = jnp.where(kk == 2, 1 - e, e)
        return a, h, part

    def by_next(k):
        return k == 2

    def own_goes(k, o):
        return has_next, jnp.logical_and(jnp.logical_and(has_next2, o > 0), jnp.logical_not(by_next(k))), o < 3

    def pass_goes(k, o):
        return (
            jnp.logical_and(jnp.logical_and(has_prev, has_next), jnp.logical_and(o > 0, by_next(k))),
            jnp.logical_and(has_back, jnp.logical_and(o > 0, jnp.logical_not(by_next(k)))),
        )

    def head_norm(v, which, hd):
        scaled = v * lax.rsqrt(jnp.mean(v * v, axis=-1, keepdims=True) + EPSILON)
        at = pl.ds(pl.multiple_of(zlo * cols + hd * HEAD_DIM, 128), HEAD_DIM)
        return (scaled * gain[which:which + 1, at]).astype(jnp.bfloat16)

    def own_pair(kk, carry):
        subs = [sub_of(2 * kk), sub_of(2 * kk + 1)]
        p = subs[0][0]
        o = 2 * p + core
        @pl.when(kk > 0)
        def _():
            for n, (_, h, part) in enumerate(subs):
                hid_wait(p, h, part)

                @pl.when(kk == 1)
                def _():
                    hid_pass(1 - n).start()

        v = jnp.concatenate([hid[p, h, half_at(part), :] for _, h, part in subs], axis=0)
        keys = dot(v, w[1])
        values = dot(v, w[2])
        for hd in range(GROUP):
            lanes = slice(hd * HEAD_DIM, (hd + 1) * HEAD_DIM)
            normed = head_norm(keys[:, lanes], 1, hd)
            plain = values[:, lanes].astype(jnp.bfloat16)
            for n, (_, h, part) in enumerate(subs):
                kv[2, o, hd, sub_rows(h, part), :] = normed[n * half:(n + 1) * half]
                kv[2, o, GROUP + hd, sub_rows(h, part), :] = plain[n * half:(n + 1) * half]
        for n, (_, h, part) in enumerate(subs):
            for flag, copy in zip(own_goes(2 * kk + n, o), (own_next, own_back, own_share)):
                @pl.when(flag)
                def _():
                    copy(o, h, part).start()

        queries = dot(v, w[0])
        for hd in range(GROUP):
            lanes = slice(hd * HEAD_DIM, (hd + 1) * HEAD_DIM)
            normed = head_norm(queries[:, lanes], 0, hd)
            for n, (_, h, part) in enumerate(subs):
                q[hd, sub_rows(2 * p + h, part), :] = normed[n * half:(n + 1) * half]
        return carry

    def pass_sub(k, carry):
        p, h, part = sub_of(k)
        o = 2 * p + core
        go_next, go_back = pass_goes(k, o)

        @pl.when(go_back)
        def _():
            kv_wait(3, o, h, part)
            pass_back(o, h, part).start()

        @pl.when(has_prev)
        def _():
            kv_wait(1, o, h, part)

            @pl.when(go_next)
            def _():
                pass_next(o, h, part).start()

            pass_share(o, h, part).start()

        return carry

    for c in (1, 2, 0):
        w_copy(c).wait()
    ow_copy().start()
    lax.fori_loop(0, 1, own_pair, 0)

    text_keys = dot(text[...], w[1])
    text_values = dot(text[...], w[2])
    for hd in range(GROUP):
        lanes = slice(hd * HEAD_DIM, (hd + 1) * HEAD_DIM)
        tk[hd] = head_norm(text_keys[:, lanes], 1, hd)
        tk[GROUP + hd] = text_values[:, lanes].astype(jnp.bfloat16)

    lax.fori_loop(0, 2, pass_sub, 0)
    lax.fori_loop(1, 2, own_pair, 0)
    lax.fori_loop(2, 4, pass_sub, 0)
    lax.fori_loop(2, 3, own_pair, 0)

    piece_rows = width // 2 // (2 * depth)

    def piece(n):
        return pl.ds(pl.multiple_of(n * piece_rows, 16), piece_rows)

    my_piece = 2 * y + core

    def ow_cross(which=None):
        of = tok if which is None else which
        return remote(
            ow.at[tok, piece(my_piece), :], ow.at[of, piece(my_piece), :],
            ow_send.at[0], ow_recv.at[my_piece], dev(line, 3 - z, core),
        )

    def ow_along(d):
        return remote(
            ow.at[1 - tok, piece(my_piece), :], ow.at[1 - tok, piece(my_piece), :],
            ow_send.at[d], ow_recv.at[my_piece], dev(4 * ((y + d) % depth) + x, z, core),
        )

    def ow_share(d, which):
        n = 2 * ((y + d) % depth) + which
        return remote(
            ow.at[1 - tok, piece(n), :], ow.at[1 - tok, piece(n), :],
            ow_send.at[depth + d], ow_recv.at[n], beside,
        )


    win_copy.wait()

    size = 2 * rows

    def attend(keys, values, spans, text_keys=False):
        ats = [pl.ds(pl.multiple_of(a * size, size), size) for a, _ in spans]
        for hd in range(GROUP):
            s = dot_t(jnp.concatenate([q[hd, at, :] for at in ats], axis=0), keys(hd))
            if text_keys:
                s = jnp.where(lax.broadcasted_iota(jnp.int32, s.shape, 1) < count[0], s, LOW)
            weights, shrinks = [], []
            for n, (_, low) in enumerate(spans):
                part = s[n * size:(n + 1) * size]
                m = jnp.broadcast_to(jnp.max(part, axis=1, keepdims=True) * SCALE, (size, HEAD_DIM))
                if not text_keys:
                    before = top[hd, ats[n], :]
                    m = jnp.maximum(before, m + low)
                    shrinks.append(jnp.exp2(before - m))
                top[hd, ats[n], :] = m
                if not text_keys:
                    m = m - low
                e = [jnp.exp2(part[:, c:c + HEAD_DIM] * SCALE - m) for c in range(0, s.shape[1], HEAD_DIM)]
                total = functools.reduce(jnp.add, e)
                tot[hd, ats[n], :] = total if text_keys else tot[hd, ats[n], :] * shrinks[n] + total
                weights.append(jnp.concatenate([v.astype(jnp.bfloat16) for v in e], axis=1))
            summed = dot(jnp.concatenate(weights, axis=0), values(hd))
            for n, at in enumerate(ats):
                part = summed[n * size:(n + 1) * size]
                acc[hd, at, :] = part if text_keys else acc[hd, at, :] * shrinks[n] + part

    def text_attend(a):
        attend(lambda hd: tk[hd], lambda hd: tk[GROUP + hd], [(a, 0.0)], text_keys=True)

    def frame_attend(g, o, *queries):
        frame = (4 * (line - 2) + 4 * g + o).astype(jnp.float32)

        def low(a):
            inside = jnp.logical_and(frame >= win[a, 0, :1], frame < win[a, 1, :1])
            return jnp.where(inside, 0.0, LOW)

        attend(lambda hd: kv[g, o, hd], lambda hd: kv[g, o, GROUP + hd], [(a, low(a)) for a in queries])

    def frame_wait(g, o):
        for n in range(4):
            kv_wait(g, o, n // 2, n % 2)

    def shared(i):
        return 2 * i + partner < 3

    def soon(i):
        return jnp.where(i < 2, 2, 1), 2 * a_soon + (core + i) % 2

    def late(i):
        return jnp.where(i < 2, 2, 1), 2 * a_late + (core + i) % 2

    def reaches(g, o, a):
        return jnp.where(g == 2, o <= 2 * a + core, has_prev)

    text_attend(a_soon)

    def first(i, carry):
        g, o = soon(i)

        @pl.when(i == 2)
        def _():
            pass_sub(4, 0)
            pass_sub(5, 0)

        @pl.when(jnp.logical_or(jnp.logical_and(i == 1, shared(a_soon)), jnp.logical_and(i == 3, has_prev)))
        def _():
            frame_wait(g, o)

        @pl.when(reaches(g, o, a_soon))
        def _():
            frame_attend(g, o, a_soon)

        return carry

    lax.fori_loop(0, 4, first, 0)
    lax.fori_loop(3, 4, own_pair, 0)
    ow_copy().wait()
    ow_cross().start()
    text_attend(a_late)

    def second(i, carry):
        g_soon, o_soon = soon(i)
        _, o_late = late(i % 2)
        early = i < 4
        g = jnp.where(early, g_soon, 2)
        o = jnp.where(early, o_soon, o_late)
        a = jnp.where(i < 6, a_late, a_soon)

        @pl.when(i == 5)
        def _():
            pass_sub(6, 0)

        @pl.when(i == 7)
        def _():
            pass_sub(7, 0)

        @pl.when(jnp.logical_and(i == 5, shared(a_late)))
        def _():
            frame_wait(g, o)

        @pl.when(reaches(g, o, a))
        def _():
            frame_attend(g, o, a)

        return carry

    lax.fori_loop(0, 8, second, 0)
    ow_cross(1 - tok).wait_recv()
    for d in range(1, depth):
        ow_along(d).start()
    ow_share(0, core).start()

    def third(i, carry):
        g, o = late(i)

        @pl.when(has_prev)
        def _():
            @pl.when(i == 3)
            def _():
                frame_wait(g, o)

            frame_attend(g, o, 0, 1)

        return carry

    lax.fori_loop(2, 4, third, 0)

    def att_copy(p, h):
        return remote(
            att.at[p, h], attin.at[z], att_send.at[p, h], att_recv.at[z], dev(line, 2 * h + p, core)
        )

    def is_here(p, h):
        return 2 * h + p == z

    def finish(p):
        for hd in range(GROUP):
            lanes = slice(hd * HEAD_DIM, (hd + 1) * HEAD_DIM)
            at = slice(p * 2 * rows, (p + 1) * 2 * rows)
            total = jnp.sum(tot[hd, at, :], axis=1, keepdims=True)
            result = (acc[hd, at, :] / total).astype(jnp.bfloat16)
            for h in range(2):
                att[p, h, :, lanes] = result[h * rows:(h + 1) * rows]
        for h in range(2):
            here = is_here(p, h)

            @pl.when(jnp.logical_not(here))
            def _():
                att_copy(p, h).start()

            @pl.when(here)
            def _():
                attin[z] = att[p, h]

    has_old = line >= 2

    @pl.when(core == 1)
    def _():
        finish(1)

    @pl.when(has_old)
    def _():
        for n in range(4):
            h, part = n // 2, n % 2
            kv_wait(0, 2 + core, h, part)
            old_share(h, part).start()
        frame_attend(0, 2 + core, 0)

    @pl.when(jnp.logical_and(has_old, core == 0))
    def _():
        frame_wait(0, 3)
        frame_attend(0, 3, 0, 1)

    @pl.when(core == 0)
    def _():
        finish(1)

    @pl.when(has_old)
    def _():
        o = 1 + core
        frame_wait(0, o)
        frame_attend(0, o, 0)

    finish(0)

    for d in range(1, depth):
        n = 2 * ((y + d) % depth) + core
        remote(
            ow.at[1 - tok, piece(n), :], ow.at[1 - tok, piece(n), :], ow_send.at[d], ow_recv.at[n], beside
        ).wait_recv()
        ow_share(d, core).start()
    for d in range(depth):
        ow_share(d, partner).wait_recv()

    for s in range(4):
        @pl.when(s != z)
        def _():
            remote(att.at[0, 0], attin.at[s], att_send.at[0, 0], att_recv.at[s], beside).wait_recv()

    step_cols = 256

    def project(n, carry):
        at = pl.ds(pl.multiple_of(n * step_cols, step_cols), step_cols)
        update = dot(attin[0], ow[0, :cols, at])
        update += dot(attin[1], ow[0, cols:, at])
        update += dot(attin[2], ow[1, :cols, at])
        update += dot(attin[3], ow[1, cols:, at])
        out[:, at] = (tokens[:, at].astype(jnp.float32) + mod[0, 2:3, at] * update).astype(jnp.bfloat16)
        return carry

    lax.fori_loop(0, width // step_cols, project, 0)

    for n in range(2):
        hid_copy(n, 0).wait_send()
        hid_copy(n, 1).wait_send()
        hid_pass(n).wait_send()

    ow_cross().wait_send()
    for d in range(1, depth):
        ow_along(d).wait_send()
    for d in range(depth):
        ow_share(d, core).wait_send()

    for p in range(2):
        for h in range(2):
            @pl.when(jnp.logical_not(is_here(p, h)))
            def _():
                att_copy(p, h).wait_send()

    def drain(k, carry):
        p, h, part = sub_of(k)
        o = 2 * p + core
        for flag, copy in zip(own_goes(k, o), (own_next, own_back, own_share)):
            @pl.when(flag)
            def _():
                copy(o, h, part).wait_send()

        for flag, copy in zip(pass_goes(k, o), (pass_next, pass_back)):
            @pl.when(flag)
            def _():
                copy(o, h, part).wait_send()

        @pl.when(has_prev)
        def _():
            pass_share(o, h, part).wait_send()

        @pl.when(jnp.logical_and(has_old, p == 0))
        def _():
            old_share(h, part).wait_send()

        return carry

    lax.fori_loop(0, 8, drain, 0)


def shards(groups, tokens, modulation, qkv_weight, out_weight, qk_gain, text, text_count, window):
    rows, width = tokens.shape
    text_rows = text.shape[0]
    cols = GROUP * HEAD_DIM
    depth = max(groups // 4, 1)
    bf16, f32 = jnp.bfloat16, jnp.float32
    vmem = pl.BlockSpec(memory_space=pltpu.VMEM)
    smem = pl.BlockSpec(memory_space=pltpu.SMEM)
    hbm = pl.BlockSpec(memory_space=pl.ANY)
    dma = pltpu.SemaphoreType.DMA
    return pl.pallas_call(
        functools.partial(kernel, groups),
        out_shape=jax.ShapeDtypeStruct((rows, width), bf16),
        in_specs=[vmem, vmem, hbm, hbm, vmem, vmem, smem, smem],
        out_specs=vmem,
        scratch_shapes=[
            pltpu.VMEM((2, 2, rows, width), bf16),
            pltpu.VMEM((2, 8, HEAD_DIM), f32),
            pltpu.VMEM((2, 2, 8, HEAD_DIM), f32),
            pltpu.VMEM((3, width, cols), bf16),
            pltpu.VMEM((2, width // 2, width), bf16),
            pltpu.VMEM((4, 4, 2 * GROUP, 2 * rows, HEAD_DIM), bf16),
            pltpu.VMEM((2 * GROUP, text_rows, HEAD_DIM), bf16),
            pltpu.VMEM((GROUP, 4 * rows, HEAD_DIM), bf16),
            pltpu.VMEM((GROUP, 4 * rows, HEAD_DIM), f32),
            pltpu.VMEM((GROUP, 4 * rows, HEAD_DIM), f32),
            pltpu.VMEM((GROUP, 4 * rows, HEAD_DIM), f32),
            pltpu.VMEM((2, 2, rows, cols), bf16),
            pltpu.VMEM((4, rows, cols), bf16),
            dma((4,)),
            dma((2, 2)),
            dma((2,)),
            dma((2, 2, 2)),
            dma,
            dma,
            dma((7, 4, 4)),
            dma((4, 4, 4)),
            dma((2 * depth,)),
            dma((2 * depth,)),
            dma((2, 2)),
            dma((4,)),
        ],
        compiler_params=pltpu.CompilerParams(
            collective_id=0, has_side_effects=True, vmem_limit_bytes=58 * 1024 * 1024
        ),
        cost_estimate=pl.CostEstimate(flops=13_000_000_000, bytes_accessed=12_000_000, transcendentals=13_400_000),
    )(tokens, modulation, qkv_weight, out_weight, qk_gain, text, text_count, window)


def solution(mesh):
    in_specs = (
        P(("frame", "tok"), None),
        P("frame", None, None),
        P(None, None, "tok"),
        P("tok", None),
        P(None, "tok"),
        P(),
        P(),
        P("frame", None),
    )
    out_specs = P(("frame", "tok"), None)
    return jax.shard_map(
        functools.partial(shards, mesh.shape["frame"] // 4),
        mesh=mesh, in_specs=in_specs, out_specs=out_specs, check_vma=False,
    )
```

```python
import functools

import jax
import jax.numpy as jnp
from jax import lax
from jax.experimental import pallas as pl
from jax.experimental.pallas import tpu as pltpu
from jax.sharding import PartitionSpec as P

HEAD_DIM = 128
GROUP = 3
EPSILON = 1e-06
LOW = -1e30
SCALE = HEAD_DIM ** (-0.5) * 1.4426950408889634
MESH = pl.DeviceIdType.MESH


def dot(a, b):
    return jnp.dot(a, b, preferred_element_type=jnp.float32)


def dot_t(a, b):
    return lax.dot_general(a, b, (((1,), (1,)), ((), ())), preferred_element_type=jnp.float32)


def kernel(
    groups,
    tokens, mod, w_hbm, ow_hbm, gain, text, count, window,
    out,
    hid, win_mine, win, w, ow, kv, tk, q, acc, top, tot, att, attin,
    w_sem, hid_send, hid_relay, hid_recv, win_send, win_recv, kv_send, kv_recv, ow_send, ow_recv, att_send, att_recv,
):
    rows, width = tokens.shape
    half = rows // 2
    cols = GROUP * HEAD_DIM
    depth = max(groups // 4, 1)
    fi = lax.axis_index("frame")
    tok = lax.axis_index("tok")
    line = fi // 4
    x = line % 4
    y = line // 4
    zlo = (fi // 2) % 2
    core = fi % 2
    z = 2 * tok + zlo
    partner = 1 - core
    a_late, a_soon = zlo, 1 - zlo

    def dev(line_, z_, core_):
        return (4 * line_ + 2 * (z_ % 2) + core_, z_ // 2)

    def remote(src, dst, send, recv, device):
        return pltpu.make_async_remote_copy(
            src_ref=src, dst_ref=dst, send_sem=send, recv_sem=recv, device_id=device, device_id_type=MESH
        )

    beside = dev(line, z, partner)
    has_prev = line > 0
    has_next = line < groups - 1
    has_next2 = line < groups - 2
    back_line = jnp.where(x == 1, line - 1, line + 3)
    back_from = jnp.where(x == 0, line + 1, line - 3)
    has_back = jnp.logical_and(back_from >= 0, back_from < groups - 2)

    def w_copy(c):
        return pltpu.make_async_copy(
            w_hbm.at[c, :, pl.ds(pl.multiple_of(zlo * cols, 128), cols)], w.at[c], w_sem.at[c]
        )

    def ow_copy():
        return pltpu.make_async_copy(ow_hbm, ow.at[tok], w_sem.at[3])

    for c in (1, 2, 0):
        w_copy(c).start()

    barrier = pltpu.get_barrier_semaphore()

    def greet(device):
        pl.semaphore_signal(barrier, inc=1, device_id=device, device_id_type=MESH)

    for c in range(2):
        for d in range(1, 4):
            greet(dev(line, (z + d) % 4, c))
    greet(beside)

    for d in range(1, depth):
        greet(dev(4 * ((y + d) % depth) + x, z, core))

    def greet_line(line_):
        for c in range(2):
            greet(dev(line_, z, c))

    @pl.when(has_prev)
    def _():
        greet_line(line - 1)

    @pl.when(has_next)
    def _():
        greet_line(line + 1)

    @pl.when(has_next2)
    def _():
        greet(dev(back_line, z, core))

    @pl.when(has_back)
    def _():
        greet(dev(back_from, z, core))
        greet_line(back_from + 2)

    old_x = (line + 2) % 4
    old_relay = jnp.where(old_x == 1, line - 3, line + 1)

    @pl.when(line >= 2)
    def _():
        greet_line(old_relay)

    def ones(flag, n):
        return jnp.where(flag, n, 0)

    greeted = (
        7 + depth - 1 + ones(has_prev, 2) + ones(has_next, 2) + ones(has_next2, 1) + ones(has_back, 3) + ones(line >= 2, 2)
    )

    step_rows = 32

    def norm_rows(step, carry):
        at = pl.ds(pl.multiple_of(step * step_rows, step_rows), step_rows)
        v = tokens[at, :].astype(jnp.float32)
        v = v - jnp.mean(v, axis=-1, keepdims=True)
        spread = jnp.mean(v * v, axis=-1, keepdims=True)
        v = v * lax.rsqrt(spread + EPSILON)
        hid[zlo, tok, at, :] = (v * (1.0 + mod[0, 1:2, :]) + mod[0, 0:1, :]).astype(jnp.bfloat16)
        return carry

    lax.fori_loop(0, rows // step_rows, norm_rows, 0)
    for n in range(2):
        win_mine[n] = jnp.full((8, HEAD_DIM), window[0, n], jnp.int32).astype(jnp.float32)

    pl.semaphore_wait(barrier, greeted)

    def half_at(part):
        return pl.ds(pl.multiple_of(part * half, half), half)

    half_below = ((z + 3) % 4) // 2
    half_above = ((z + 1) % 4) // 2

    def hid_copy(up, part):
        at = half_at(part)
        return remote(
            hid.at[zlo, tok, at, :], hid.at[zlo, tok, at, :],
            hid_send.at[up, part], hid_recv.at[zlo, tok, part], dev(line, (z + (1 if up else 3)) % 4, core),
        )

    win_copy = remote(win_mine, win.at[zlo], win_send, win_recv, dev(line, (z + 1) % 4, core))

    def hid_wait(a, h, part):
        at = half_at(part)
        remote(
            hid.at[a, h, at, :], hid.at[a, h, at, :], hid_send.at[0, part], hid_recv.at[a, h, part], beside
        ).wait_recv()

    def hid_pass(up):
        h, part = (half_below, 0) if up else (half_above, 1)
        at = half_at(part)
        return remote(
            hid.at[a_soon, h, at, :], hid.at[a_soon, h, at, :],
            hid_relay.at[up], hid_recv.at[a_soon, h, part], dev(line, (z + (1 if up else 3)) % 4, core),
        )

    hid_copy(1, 0).start()
    hid_copy(0, 1).start()
    hid_copy(1, 1).start()
    hid_copy(0, 0).start()
    win_copy.start()
    win[zlo] = win_mine[...]

    def sub_rows(h, part):
        return pl.ds(pl.multiple_of((2 * h + part) * half, half), half)

    def kv_copy(kind, g, o, h, part, to_g, device):
        at = sub_rows(h, part)
        return remote(
            kv.at[g, o, :, at, :], kv.at[to_g, o, :, at, :],
            kv_send.at[kind, o, 2 * h + part], kv_recv.at[to_g, o, 2 * h + part], device,
        )

    def kv_wait(g, o, h, part):
        kv_copy(0, g, o, h, part, g, beside).wait_recv()

    def old_core(o):
        return jnp.where(o == 3, 1, 0)

    def own_next(o, h, part):
        return kv_copy(0, 2, o, h, part, 1, dev(line + 1, z, core))

    def own_back(o, h, part):
        return kv_copy(1, 2, o, h, part, 3, dev(back_line, z, core))

    def own_share(o, h, part):
        return kv_copy(2, 2, o, h, part, 2, beside)

    def pass_next(o, h, part):
        return kv_copy(3, 1, o, h, part, 0, dev(line + 1, z, old_core(o)))

    def pass_share(o, h, part):
        return kv_copy(4, 1, o, h, part, 1, beside)

    def pass_back(o, h, part):
        return kv_copy(5, 3, o, h, part, 0, dev(back_from + 2, z, old_core(o)))

    def old_share(h, part):
        return kv_copy(6, 0, 2 + core, h, part, 0, beside)

    def sub_of(k):
        kk, e = k // 2, k % 2
        outer = jnp.logical_or(kk == 0, kk == 3)
        a = jnp.where(outer, a_late, a_soon)
        h = jnp.where(outer, (tok + kk // 3) % 2, jnp.where(e == 0, half_below, half_above))
        part = jnp.where(kk == 2, 1 - e, e)
        return a, h, part

    def by_next(k):
        return k > 99

    def own_goes(k, o):
        return has_next, jnp.logical_and(jnp.logical_and(has_next2, o > 0), jnp.logical_not(by_next(k))), o < 3

    def pass_goes(k, o):
        return (
            jnp.logical_and(jnp.logical_and(has_prev, has_next), jnp.logical_and(o > 0, by_next(k))),
            jnp.logical_and(has_back, jnp.logical_and(o > 0, jnp.logical_not(by_next(k)))),
        )

    def head_norm(v, which, hd):
        scaled = v * lax.rsqrt(jnp.mean(v * v, axis=-1, keepdims=True) + EPSILON)
        at = pl.ds(pl.multiple_of(zlo * cols + hd * HEAD_DIM, 128), HEAD_DIM)
        return (scaled * gain[which:which + 1, at]).astype(jnp.bfloat16)

    def own_pair(kk, carry):
        subs = [sub_of(2 * kk), sub_of(2 * kk + 1)]
        p = subs[0][0]
        o = 2 * p + core
        @pl.when(kk > 0)
        def _():
            for n, (_, h, part) in enumerate(subs):
                hid_wait(p, h, part)

                @pl.when(kk == 1)
                def _():
                    hid_pass(1 - n).start()

        v = jnp.concatenate([hid[p, h, half_at(part), :] for _, h, part in subs], axis=0)
        keys = dot(v, w[1])
        values = dot(v, w[2])
        for hd in range(GROUP):
            lanes = slice(hd * HEAD_DIM, (hd + 1) * HEAD_DIM)
            normed = head_norm(keys[:, lanes], 1, hd)
            plain = values[:, lanes].astype(jnp.bfloat16)
            for n, (_, h, part) in enumerate(subs):
                kv[2, o, hd, sub_rows(h, part), :] = normed[n * half:(n + 1) * half]
                kv[2, o, GROUP + hd, sub_rows(h, part), :] = plain[n * half:(n + 1) * half]
        for n, (_, h, part) in enumerate(subs):
            for flag, copy in zip(own_goes(2 * kk + n, o), (own_next, own_back, own_share)):
                @pl.when(flag)
                def _():
                    copy(o, h, part).start()

        queries = dot(v, w[0])
        for hd in range(GROUP):
            lanes = slice(hd * HEAD_DIM, (hd + 1) * HEAD_DIM)
            normed = head_norm(queries[:, lanes], 0, hd)
            for n, (_, h, part) in enumerate(subs):
                q[hd, sub_rows(2 * p + h, part), :] = normed[n * half:(n + 1) * half]
        return carry

    def pass_sub(k, carry):
        p, h, part = sub_of(k)
        o = 2 * p + core
        go_next, go_back = pass_goes(k, o)

        @pl.when(go_back)
        def _():
            kv_wait(3, o, h, part)
            pass_back(o, h, part).start()

        @pl.when(has_prev)
        def _():
            kv_wait(1, o, h, part)

            @pl.when(go_next)
            def _():
                pass_next(o, h, part).start()

            pass_share(o, h, part).start()

        return carry

    for c in (1, 2, 0):
        w_copy(c).wait()
    ow_copy().start()
    lax.fori_loop(0, 1, own_pair, 0)

    text_keys = dot(text[...], w[1])
    text_values = dot(text[...], w[2])
    for hd in range(GROUP):
        lanes = slice(hd * HEAD_DIM, (hd + 1) * HEAD_DIM)
        tk[hd] = head_norm(text_keys[:, lanes], 1, hd)
        tk[GROUP + hd] = text_values[:, lanes].astype(jnp.bfloat16)

    lax.fori_loop(0, 2, pass_sub, 0)
    lax.fori_loop(1, 2, own_pair, 0)
    lax.fori_loop(2, 4, pass_sub, 0)
    lax.fori_loop(2, 3, own_pair, 0)

    piece_rows = width // 2 // (2 * depth)

    def piece(n):
        return pl.ds(pl.multiple_of(n * piece_rows, 16), piece_rows)

    my_piece = 2 * y + core

    def ow_cross(which=None):
        of = tok if which is None else which
        return remote(
            ow.at[tok, piece(my_piece), :], ow.at[of, piece(my_piece), :],
            ow_send.at[0], ow_recv.at[my_piece], dev(line, 3 - z, core),
        )

    def ow_along(d):
        return remote(
            ow.at[1 - tok, piece(my_piece), :], ow.at[1 - tok, piece(my_piece), :],
            ow_send.at[d], ow_recv.at[my_piece], dev(4 * ((y + d) % depth) + x, z, core),
        )

    def ow_share(d, which):
        n = 2 * ((y + d) % depth) + which
        return remote(
            ow.at[1 - tok, piece(n), :], ow.at[1 - tok, piece(n), :],
            ow_send.at[depth + d], ow_recv.at[n], beside,
        )


    win_copy.wait()

    size = 2 * rows

    def attend(keys, values, spans, text_keys=False):
        ats = [pl.ds(pl.multiple_of(a * size, size), size) for a, _ in spans]
        for hd in range(GROUP):
            s = dot_t(jnp.concatenate([q[hd, at, :] for at in ats], axis=0), keys(hd))
            if text_keys:
                s = jnp.where(lax.broadcasted_iota(jnp.int32, s.shape, 1) < count[0], s, LOW)
            weights, shrinks = [], []
            for n, (_, low) in enumerate(spans):
                part = s[n * size:(n + 1) * size]
                m = jnp.broadcast_to(jnp.max(part, axis=1, keepdims=True) * SCALE, (size, HEAD_DIM))
                if not text_keys:
                    before = top[hd, ats[n], :]
                    m = jnp.maximum(before, m + low)
                    shrinks.append(jnp.exp2(before - m))
                top[hd, ats[n], :] = m
                if not text_keys:
                    m = m - low
                e = [jnp.exp2(part[:, c:c + HEAD_DIM] * SCALE - m) for c in range(0, s.shape[1], HEAD_DIM)]
                total = functools.reduce(jnp.add, e)
                tot[hd, ats[n], :] = total if text_keys else tot[hd, ats[n], :] * shrinks[n] + total
                weights.append(jnp.concatenate([v.astype(jnp.bfloat16) for v in e], axis=1))
            summed = dot(jnp.concatenate(weights, axis=0), values(hd))
            for n, at in enumerate(ats):
                part = summed[n * size:(n + 1) * size]
                acc[hd, at, :] = part if text_keys else acc[hd, at, :] * shrinks[n] + part

    def text_attend(a):
        attend(lambda hd: tk[hd], lambda hd: tk[GROUP + hd], [(a, 0.0)], text_keys=True)

    def frame_attend(g, o, *queries):
        frame = (4 * (line - 2) + 4 * g + o).astype(jnp.float32)

        def low(a):
            inside = jnp.logical_and(frame >= win[a, 0, :1], frame < win[a, 1, :1])
            return jnp.where(inside, 0.0, LOW)

        attend(lambda hd: kv[g, o, hd], lambda hd: kv[g, o, GROUP + hd], [(a, low(a)) for a in queries])

    def frame_wait(g, o):
        for n in range(4):
            kv_wait(g, o, n // 2, n % 2)

    def shared(i):
        return 2 * i + partner < 3

    def soon(i):
        return jnp.where(i < 2, 2, 1), 2 * a_soon + (core + i) % 2

    def late(i):
        return jnp.where(i < 2, 2, 1), 2 * a_late + (core + i) % 2

    def reaches(g, o, a):
        return jnp.where(g == 2, o <= 2 * a + core, has_prev)

    text_attend(a_soon)

    def first(i, carry):
        g, o = soon(i)

        @pl.when(i == 2)
        def _():
            pass_sub(4, 0)
            pass_sub(5, 0)

        @pl.when(jnp.logical_or(jnp.logical_and(i == 1, shared(a_soon)), jnp.logical_and(i == 3, has_prev)))
        def _():
            frame_wait(g, o)

        @pl.when(reaches(g, o, a_soon))
        def _():
            frame_attend(g, o, a_soon)

        return carry

    lax.fori_loop(0, 4, first, 0)
    lax.fori_loop(3, 4, own_pair, 0)
    ow_copy().wait()
    ow_cross().start()
    text_attend(a_late)

    def second(i, carry):
        g_soon, o_soon = soon(i)
        _, o_late = late(i % 2)
        early = i < 4
        g = jnp.where(early, g_soon, 2)
        o = jnp.where(early, o_soon, o_late)
        a = jnp.where(i < 6, a_late, a_soon)

        @pl.when(i == 5)
        def _():
            pass_sub(6, 0)

        @pl.when(i == 7)
        def _():
            pass_sub(7, 0)

        @pl.when(jnp.logical_and(i == 5, shared(a_late)))
        def _():
            frame_wait(g, o)

        @pl.when(reaches(g, o, a))
        def _():
            frame_attend(g, o, a)

        return carry

    lax.fori_loop(0, 8, second, 0)
    ow_cross(1 - tok).wait_recv()
    for d in range(1, depth):
        ow_along(d).start()
    ow_share(0, core).start()

    def third(i, carry):
        g, o = late(i)

        @pl.when(has_prev)
        def _():
            @pl.when(i == 3)
            def _():
                frame_wait(g, o)

            frame_attend(g, o, 0, 1)

        return carry

    lax.fori_loop(2, 4, third, 0)

    def att_copy(p, h):
        return remote(
            att.at[p, h], attin.at[z], att_send.at[p, h], att_recv.at[z], dev(line, 2 * h + p, core)
        )

    def is_here(p, h):
        return 2 * h + p == z

    def finish(p):
        for hd in range(GROUP):
            lanes = slice(hd * HEAD_DIM, (hd + 1) * HEAD_DIM)
            at = slice(p * 2 * rows, (p + 1) * 2 * rows)
            total = jnp.sum(tot[hd, at, :], axis=1, keepdims=True)
            result = (acc[hd, at, :] / total).astype(jnp.bfloat16)
            for h in range(2):
                att[p, h, :, lanes] = result[h * rows:(h + 1) * rows]
        for h in range(2):
            here = is_here(p, h)

            @pl.when(jnp.logical_not(here))
            def _():
                att_copy(p, h).start()

            @pl.when(here)
            def _():
                attin[z] = att[p, h]

    has_old = line >= 2

    @pl.when(core == 1)
    def _():
        finish(1)

    @pl.when(has_old)
    def _():
        for n in range(4):
            h, part = n // 2, n % 2
            kv_wait(0, 2 + core, h, part)
            old_share(h, part).start()
        frame_attend(0, 2 + core, 0)

    @pl.when(jnp.logical_and(has_old, core == 0))
    def _():
        frame_wait(0, 3)
        frame_attend(0, 3, 0, 1)

    @pl.when(core == 0)
    def _():
        finish(1)

    @pl.when(has_old)
    def _():
        o = 1 + core
        frame_wait(0, o)
        frame_attend(0, o, 0)

    finish(0)

    for d in range(1, depth):
        n = 2 * ((y + d) % depth) + core
        remote(
            ow.at[1 - tok, piece(n), :], ow.at[1 - tok, piece(n), :], ow_send.at[d], ow_recv.at[n], beside
        ).wait_recv()
        ow_share(d, core).start()
    for d in range(depth):
        ow_share(d, partner).wait_recv()

    for s in range(4):
        @pl.when(s != z)
        def _():
            remote(att.at[0, 0], attin.at[s], att_send.at[0, 0], att_recv.at[s], beside).wait_recv()

    step_cols = 256

    def project(n, carry):
        at = pl.ds(pl.multiple_of(n * step_cols, step_cols), step_cols)
        update = dot(attin[0], ow[0, :cols, at])
        update += dot(attin[1], ow[0, cols:, at])
        update += dot(attin[2], ow[1, :cols, at])
        update += dot(attin[3], ow[1, cols:, at])
        out[:, at] = (tokens[:, at].astype(jnp.float32) + mod[0, 2:3, at] * update).astype(jnp.bfloat16)
        return carry

    lax.fori_loop(0, width // step_cols, project, 0)

    for n in range(2):
        hid_copy(n, 0).wait_send()
        hid_copy(n, 1).wait_send()
        hid_pass(n).wait_send()

    ow_cross().wait_send()
    for d in range(1, depth):
        ow_along(d).wait_send()
    for d in range(depth):
        ow_share(d, core).wait_send()

    for p in range(2):
        for h in range(2):
            @pl.when(jnp.logical_not(is_here(p, h)))
            def _():
                att_copy(p, h).wait_send()

    def drain(k, carry):
        p, h, part = sub_of(k)
        o = 2 * p + core
        for flag, copy in zip(own_goes(k, o), (own_next, own_back, own_share)):
            @pl.when(flag)
            def _():
                copy(o, h, part).wait_send()

        for flag, copy in zip(pass_goes(k, o), (pass_next, pass_back)):
            @pl.when(flag)
            def _():
                copy(o, h, part).wait_send()

        @pl.when(has_prev)
        def _():
            pass_share(o, h, part).wait_send()

        @pl.when(jnp.logical_and(has_old, p == 0))
        def _():
            old_share(h, part).wait_send()

        return carry

    lax.fori_loop(0, 8, drain, 0)


def shards(groups, tokens, modulation, qkv_weight, out_weight, qk_gain, text, text_count, window):
    rows, width = tokens.shape
    text_rows = text.shape[0]
    cols = GROUP * HEAD_DIM
    depth = max(groups // 4, 1)
    bf16, f32 = jnp.bfloat16, jnp.float32
    vmem = pl.BlockSpec(memory_space=pltpu.VMEM)
    smem = pl.BlockSpec(memory_space=pltpu.SMEM)
    hbm = pl.BlockSpec(memory_space=pl.ANY)
    dma = pltpu.SemaphoreType.DMA
    return pl.pallas_call(
        functools.partial(kernel, groups),
        out_shape=jax.ShapeDtypeStruct((rows, width), bf16),
        in_specs=[vmem, vmem, hbm, hbm, vmem, vmem, smem, smem],
        out_specs=vmem,
        scratch_shapes=[
            pltpu.VMEM((2, 2, rows, width), bf16),
            pltpu.VMEM((2, 8, HEAD_DIM), f32),
            pltpu.VMEM((2, 2, 8, HEAD_DIM), f32),
            pltpu.VMEM((3, width, cols), bf16),
            pltpu.VMEM((2, width // 2, width), bf16),
            pltpu.VMEM((4, 4, 2 * GROUP, 2 * rows, HEAD_DIM), bf16),
            pltpu.VMEM((2 * GROUP, text_rows, HEAD_DIM), bf16),
            pltpu.VMEM((GROUP, 4 * rows, HEAD_DIM), bf16),
            pltpu.VMEM((GROUP, 4 * rows, HEAD_DIM), f32),
            pltpu.VMEM((GROUP, 4 * rows, HEAD_DIM), f32),
            pltpu.VMEM((GROUP, 4 * rows, HEAD_DIM), f32),
            pltpu.VMEM((2, 2, rows, cols), bf16),
            pltpu.VMEM((4, rows, cols), bf16),
            dma((4,)),
            dma((2, 2)),
            dma((2,)),
            dma((2, 2, 2)),
            dma,
            dma,
            dma((7, 4, 4)),
            dma((4, 4, 4)),
            dma((2 * depth,)),
            dma((2 * depth,)),
            dma((2, 2)),
            dma((4,)),
        ],
        compiler_params=pltpu.CompilerParams(
            collective_id=0, has_side_effects=True, vmem_limit_bytes=58 * 1024 * 1024
        ),
        cost_estimate=pl.CostEstimate(flops=13_000_000_000, bytes_accessed=12_000_000, transcendentals=13_400_000),
    )(tokens, modulation, qkv_weight, out_weight, qk_gain, text, text_count, window)


def solution(mesh):
    in_specs = (
        P(("frame", "tok"), None),
        P("frame", None, None),
        P(None, None, "tok"),
        P("tok", None),
        P(None, "tok"),
        P(),
        P(),
        P("frame", None),
    )
    out_specs = P(("frame", "tok"), None)
    return jax.shard_map(
        functools.partial(shards, mesh.shape["frame"] // 4),
        mesh=mesh, in_specs=in_specs, out_specs=out_specs, check_vma=False,
    )
```
